32 devices in a mesh: blk: 8 (over z, x), slab: 4 (over y, core).
Axes of the slice: x: 2, y: 2, z: 4, core: 2. Of those that a mesh axis runs over, the one named last changes fastest.
Arguments:
- a_tiles: bfloat16 [4096, 8192], P('blk', 'slab'), may hold values from -0.125 to 0.125
- tile_cols: int32 [16, 4, 8], P('blk', 'slab'), may hold values from 0 to 15, as said below
- tile_counts: int32 [16, 4], P('blk', 'slab'), may hold values from 1 to 8, as said below
- scaling: float32 [16384], P('slab'), may hold values from 0.1 to 10
- panel: int32 [1], replicated, may hold values from 0 to 15
Outputs:
- normal_band: float32 [4096, 3, 512], P('blk', None, 'slab')
The draws below stay inside these ranges and needn't reach their ends.
Inputs may be any that keep to these rules, and one draw needn't show every extreme that they name: `tile_cols`: the 8 column tiles listed for one row block in one slab are distinct. `tile_counts`: the largest count is 8 in every draw.
All inputs are finite; a program needn't handle non-finite values.
Results may differ from the reference program's by a relative error of at most 0.0015.
Values may be sent and summed in bfloat16 or wider, within the bound.
A program may use at most 64 MiB of HBM per device.

```python
import math
import jax
import jax.numpy as jnp
from jax import lax

TILE = 256
SLOTS = 8
COL_TILES = 16
RB_DEV = 2
BLOCKS = 16
ROWS = 4096
GROUP_W = 512
COLUMNS = 16384
N_BLK = 8
N_SLAB = 4


def draw_tile_cols(key, part):
    entries = BLOCKS * N_SLAB
    key_list = jax.random.split(jax.random.fold_in(key, 11), entries)
    orders = jax.vmap(lambda single: jax.random.permutation(single, COL_TILES))(key_list)
    return orders[:, :SLOTS].reshape(BLOCKS, N_SLAB, SLOTS).astype(jnp.int32)


def draw_tile_counts(key, part):
    first, second, third = jax.random.split(jax.random.fold_in(key, 23), 3)
    full_rows = jax.random.randint(first, (BLOCKS * N_SLAB,), 0, 20) < 3
    lower_counts = jax.random.randint(second, (BLOCKS * N_SLAB,), 1, SLOTS // 2 + 1)
    counts = jnp.where(full_rows, SLOTS, lower_counts)
    forced = jax.random.randint(third, (), 0, BLOCKS * N_SLAB)
    counts = counts.at[forced].set(SLOTS)
    return counts.reshape(BLOCKS, N_SLAB).astype(jnp.int32)


def levels(stream_key, dims, shards, smallest, largest):
    gain, own = 1.0, jax.random.fold_in(stream_key, 6)
    for position, parts in shards:
        draws = jnp.exp(jax.random.uniform(jax.random.fold_in(own, position), (parts,), jnp.float32, smallest / len(shards), largest / len(shards)))
        gain = gain * jnp.repeat(draws, dims[position] // parts).reshape([-1 if axis == position else 1 for axis in range(len(dims))])
    return gain


def centred(stream_key, shape, deviation, reach, cuts=(), held_as=jnp.bfloat16):
    array = deviation * jax.random.normal(stream_key, shape, jnp.float32)
    if cuts:
        array = array * levels(stream_key, shape, cuts, -0.22, 0.18)
    return jnp.clip(array, -reach, reach).astype(held_as)


def setup_inputs(seed: int = 0) -> dict:
    key_of = jax.random.split(jax.random.key(seed), 6)
    a_tiles = centred(key_of[0], (ROWS, N_SLAB * SLOTS * TILE), (SLOTS * TILE) ** -0.5, 0.125, ((0, 8), (1, 4)))
    tile_cols = draw_tile_cols(jax.random.fold_in(key_of[5], 71), 0)
    tile_counts = draw_tile_counts(jax.random.fold_in(key_of[5], 71), 0)
    scaling = jnp.clip(jnp.exp(math.log(10.0) - 4.6051702 * jax.random.uniform(key_of[3], (COLUMNS,), jnp.float32) ** levels(key_of[3], (COLUMNS,), ((0, 4),), -0.2, 0.2)), 0.1, 10.0)
    panel = jax.random.randint(key_of[4], (1,), 0, BLOCKS).astype(jnp.int32)
    return dict(a_tiles=a_tiles, tile_cols=tile_cols, tile_counts=tile_counts, scaling=scaling, panel=panel)


ridge_shift = 0.05

def reference(a_tiles, tile_cols, tile_counts, scaling, panel):
    blocks_five = a_tiles.reshape(BLOCKS, TILE, N_SLAB, SLOTS, TILE)
    scale_three = scaling.reshape(N_SLAB, COL_TILES, TILE)
    slot_ids = jnp.arange(SLOTS, dtype=jnp.int32)
    slab_ids = jnp.arange(N_SLAB, dtype=jnp.int32)
    live = slot_ids[None, None, :] < tile_counts[:, :, None]
    picked = scale_three[slab_ids[None, :, None], tile_cols]
    picked = jnp.where(live[..., None], picked, jnp.float32(0.0))
    scaled = (blocks_five.astype(jnp.float32) * picked[:, None]).astype(jnp.bfloat16)
    matches = (tile_cols[..., None] == jnp.arange(COL_TILES, dtype=jnp.int32)) & live[..., None]
    found = jnp.any(matches, axis=2).astype(jnp.int32)
    lookup = (jnp.sum(jnp.where(matches, slot_ids[:, None], 0), axis=2) + SLOTS * (1 - found)).astype(jnp.int32)
    padded = jnp.concatenate([blocks_five, jnp.zeros((BLOCKS, TILE, N_SLAB, 1, TILE), jnp.bfloat16)], axis=3)
    member = jnp.arange(RB_DEV, dtype=jnp.int32)
    identity = jnp.eye(TILE, dtype=jnp.float32)

    def one_row(row_block):
        group_pos = row_block // RB_DEV
        own_scaled = scaled[row_block].astype(jnp.float32)
        planes = []
        for shift_by in range(3):
            others = ((group_pos - shift_by) % N_BLK * RB_DEV + member).astype(jnp.int32)
            table = lookup[others]
            slot_index = table[:, slab_ids[:, None], tile_cols[row_block]]
            chosen = padded[others]
            aligned = chosen[member[:, None, None], :, slab_ids[None, :, None], slot_index]
            product = jnp.einsum('xsmy,bsmzy->xbz', own_scaled, aligned.astype(jnp.float32), precision=lax.Precision.HIGHEST)
            if shift_by == 0:
                diag_mask = (member == row_block % RB_DEV).astype(jnp.float32)
                product = product + ridge_shift * identity[:, None, :] * diag_mask[None, :, None]
            planes.append(product.reshape(TILE, GROUP_W))
        return jnp.stack(planes, axis=1)
    band = lax.map(one_row, jnp.arange(BLOCKS, dtype=jnp.int32)).reshape(N_BLK, GROUP_W, 3, GROUP_W)
    pivot_block = panel[0].astype(jnp.int32)
    pivot_group = (pivot_block // RB_DEV).astype(jnp.int32)
    pivot_pos = (pivot_block % RB_DEV).astype(jnp.int32)
    zero_index = jnp.int32(0)
    pivot_offset = (pivot_pos * TILE).astype(jnp.int32)
    row_blocks = jnp.arange(GROUP_W, dtype=jnp.int32) // TILE
    is_pivot = (row_blocks == pivot_pos)[:, None]
    plane_first = band[pivot_group][:, 0, :]
    column_first = lax.dynamic_slice(plane_first, (zero_index, pivot_offset), (GROUP_W, TILE))
    pivot_tile = lax.dynamic_slice(column_first, (pivot_offset, zero_index), (TILE, TILE))
    factor = jnp.linalg.cholesky(pivot_tile)
    solved_first = jax.scipy.linalg.solve_triangular(factor, column_first.T, lower=True).T
    lower_first = jnp.where(is_pivot, jnp.float32(0.0), solved_first)
    plane_first = plane_first - jnp.dot(lower_first.astype(jnp.float32), lower_first.T.astype(jnp.float32), precision=lax.Precision.HIGHEST, preferred_element_type=jnp.float32)
    stacked_factor = jnp.tile(factor, (RB_DEV, 1))
    new_first = jnp.where(is_pivot, stacked_factor, solved_first)
    plane_first = lax.dynamic_update_slice(plane_first, new_first, (zero_index, pivot_offset))
    band = band.at[pivot_group, :, 0, :].set(plane_first)
    return band.reshape(ROWS, 3, GROUP_W)
```

```python
import functools

import jax
import jax.numpy as jnp
from jax import lax
from jax.experimental import pallas as pl
from jax.experimental.pallas import tpu as pltpu
from jax.sharding import PartitionSpec as P

ridge_shift = 0.05
MESH = pl.DeviceIdType.MESH
PIECES = 8


def band_kernel(
    groups, slots, a_ref, picked_ref, meta_ref, pos_ref, band_ref, column_ref,
    scaled, aligned, one_far, one_near, two_far, two_near, meta_one, meta_two, part, landed, gathered,
    z_send, z_recv, x_send, x_recv, meta_send, meta_recv,
    sum_send, sum_recv, all_send, all_recv,
):
    rows = a_ref.shape[0]
    tile = rows // 2
    half = tile // 2
    piece = rows // PIECES
    per_block = PIECES // 2
    group = lax.axis_index("blk")
    slab = lax.axis_index("slab")
    chip = slab // 2
    core = slab % 2
    odd = group % 2
    ahead = (group + 2) % groups
    behind = (group + groups - 2) % groups
    across = group + 1 - 2 * odd
    mate = chip * 2 + 1 - core
    facing = (1 - chip) * 2 + core
    diagonal = (1 - chip) * 2 + 1 - core
    peers = (mate, facing, diagonal)
    far = 1 - chip
    near = chip

    barrier = pltpu.get_barrier_semaphore()
    for other in (ahead, behind, across):
        pl.semaphore_signal(barrier, inc=1, device_id=(other, slab), device_id_type=MESH)
    for other in peers:
        pl.semaphore_signal(barrier, inc=1, device_id=(group, other), device_id_type=MESH)
    pl.semaphore_wait(barrier, 6)

    def piece_rows(n):
        block = far if n < per_block else near
        return pl.ds(pl.multiple_of(block * tile + (n % per_block) * piece, piece), piece)

    def piece_of(far_ref, near_ref, n):
        start = n % per_block * piece
        return (far_ref if n < per_block else near_ref).at[start:start + piece]

    def to_ahead(n):
        return pltpu.make_async_remote_copy(
            src_ref=a_ref.at[piece_rows(n)], dst_ref=piece_of(two_far, two_near, n),
            send_sem=z_send.at[n], recv_sem=z_recv.at[n],
            device_id=(ahead, slab), device_id_type=MESH)

    def to_across(n, source):
        return pltpu.make_async_remote_copy(
            src_ref=source, dst_ref=piece_of(one_far, one_near, n),
            send_sem=x_send.at[n], recv_sem=x_recv.at[n],
            device_id=(across, slab), device_id_type=MESH)

    def meta_ahead():
        return pltpu.make_async_remote_copy(
            src_ref=meta_ref, dst_ref=meta_two, send_sem=meta_send.at[0], recv_sem=meta_recv.at[0],
            device_id=(ahead, slab), device_id_type=MESH)

    def meta_across(source):
        return pltpu.make_async_remote_copy(
            src_ref=source, dst_ref=meta_one, send_sem=meta_send.at[1], recv_sem=meta_recv.at[1],
            device_id=(across, slab), device_id_type=MESH)

    meta_ahead().start()
    for n in range(PIECES):
        to_ahead(n).start()

    @pl.when(odd == 0)
    def _():
        meta_across(meta_ref).start()
        for n in range(PIECES):
            to_across(n, a_ref.at[piece_rows(n)]).start()

    def scale_slot(i, m):
        where = (pl.ds(i * tile, tile), pl.ds(m * tile, tile))
        factors = picked_ref[i * slots + m:i * slots + m + 1, :]
        scaled[where] = (a_ref[where].astype(jnp.float32) * factors).astype(jnp.bfloat16)

    for i in range(2):
        for m in range(slots):
            scale_slot(i, m)

    def sum_copy(plane, d):
        return pltpu.make_async_remote_copy(
            src_ref=part.at[plane, peers[d]], dst_ref=landed.at[plane, d],
            send_sem=sum_send.at[plane, d], recv_sem=sum_recv.at[plane, d],
            device_id=(group, peers[d]), device_id_type=MESH)

    def multiply(plane, block, source, other_meta):
        first = pl.ds(0, tile)
        if plane == 0:
            first = pl.ds(pl.multiple_of(block * tile, tile), tile)

        def align(i):
            def one_slot(m, carry):
                mine = meta_ref[pl.ds(i * slots + m, 1), :]
                total = jnp.zeros((tile, tile), jnp.bfloat16)
                for n in range(slots):
                    theirs = other_meta[pl.ds(block * slots + n, 1), :]
                    same = jnp.where(mine == theirs, jnp.float32(1.0), jnp.float32(0.0))
                    same = jnp.concatenate([same, same], axis=1).astype(jnp.bfloat16)
                    total += source[first, n * tile:(n + 1) * tile] * same
                aligned[:, pl.ds(pl.multiple_of(m * tile, tile), tile)] = total
                return carry

            lax.fori_loop(0, slots, one_slot, 0)
            return aligned[...]

        def one(i, direct):
            here = pl.ds(pl.multiple_of(i * tile, tile), tile)
            other = source[first, :] if direct else align(i)
            total = lax.dot_general(
                scaled[here, :], other, (((1,), (1,)), ((), ())),
                preferred_element_type=jnp.float32)
            part[plane, 2 * block, here] = total[:, :half]
            part[plane, 2 * block + 1, here] = total[:, half:]

        one(block, plane == 0)
        one(1 - block, False)
        if block is far:
            sum_copy(plane, 1).start()
            sum_copy(plane, 2).start()
        else:
            sum_copy(plane, 0).start()

    def forward(n):
        to_ahead(n).wait_recv()

        @pl.when(odd == 1)
        def _():
            to_across(n, piece_of(two_far, two_near, n)).start()

    multiply(0, far, a_ref, meta_ref)
    multiply(0, near, a_ref, meta_ref)

    meta_ahead().wait_recv()

    @pl.when(odd == 1)
    def _():
        meta_across(meta_two).start()

    forward(0)
    meta_across(meta_ref).wait_recv()

    for d in range(3):
        sum_copy(0, d).wait_recv()
    row_ids = lax.broadcasted_iota(jnp.int32, (rows, half), 0)
    col_ids = lax.broadcasted_iota(jnp.int32, (rows, half), 1) + slab * half
    ridge = jnp.where(row_ids == col_ids, jnp.float32(ridge_shift), jnp.float32(0.0))
    gathered[slab] = (part[0, slab] + landed[0, 0]) + (landed[0, 1] + landed[0, 2]) + ridge

    def all_copy(d):
        return pltpu.make_async_remote_copy(
            src_ref=gathered.at[slab], dst_ref=gathered.at[slab],
            send_sem=all_send.at[d], recv_sem=all_recv.at[d],
            device_id=(group, peers[d]), device_id_type=MESH)

    def all_arrival(d):
        return pltpu.make_async_remote_copy(
            src_ref=gathered.at[slab], dst_ref=gathered.at[peers[d]],
            send_sem=all_send.at[d], recv_sem=all_recv.at[d],
            device_id=(group, peers[d]), device_id_type=MESH)

    for d in (1, 2, 0):
        all_copy(d).start()
    band_ref[0] = gathered[slab]

    for n in range(1, per_block):
        forward(n)
    multiply(2, far, two_far, meta_two)
    for n in range(per_block):
        to_across(n, piece_of(two_far, two_near, n)).wait_recv()
    multiply(1, far, one_far, meta_one)

    for d in range(3):
        all_arrival(d).wait_recv()
    first_half = pos_ref[0:1, :] == 0
    for h in range(2):
        column_ref[:, h * half:(h + 1) * half] = jnp.where(
            first_half, gathered[h], gathered[2 + h])

    for n in range(per_block, PIECES):
        forward(n)
    multiply(2, near, two_near, meta_two)
    for n in range(per_block, PIECES):
        to_across(n, piece_of(two_far, two_near, n)).wait_recv()
    multiply(1, near, one_near, meta_one)
    for plane in (2, 1):
        for d in range(3):
            sum_copy(plane, d).wait_recv()
        band_ref[plane] = (part[plane, slab] + landed[plane, 0]) + (
            landed[plane, 1] + landed[plane, 2])

    meta_ahead().wait_send()
    meta_across(meta_ref).wait_send()
    for n in range(PIECES):
        to_ahead(n).wait_send()
        to_across(n, piece_of(two_far, two_near, n)).wait_send()
    for d in range(3):
        all_copy(d).wait_send()
        for plane in range(3):
            sum_copy(plane, d).wait_send()


def body(a_tiles, tile_cols, tile_counts, scaling, panel):
    rows = a_tiles.shape[0]
    blocks_here = tile_cols.shape[0]
    slots = tile_cols.shape[2]
    tile = rows // blocks_here
    half = rows // 4
    col_tiles = scaling.shape[0] // tile
    groups = lax.axis_size("blk")
    group_pos = lax.axis_index("blk")
    slab_pos = lax.axis_index("slab")
    cols = tile_cols[:, 0, :]
    slot_ids = jnp.arange(slots, dtype=jnp.int32)
    live = slot_ids[None, :] < tile_counts
    picked = jnp.where(live[..., None], scaling.reshape(col_tiles, tile)[cols], jnp.float32(0.0))
    picked = picked.reshape(blocks_here * slots, tile)
    meta = jnp.where(live, cols, -1).reshape(blocks_here * slots, 1)
    meta = jnp.broadcast_to(meta, (blocks_here * slots, half))
    positions = jnp.full((8, half), panel[0] % blocks_here, jnp.int32)
    vmem = pl.BlockSpec(memory_space=pltpu.VMEM)
    dma = pltpu.SemaphoreType.DMA
    band, column = pl.pallas_call(
        functools.partial(band_kernel, groups, slots),
        out_shape=(
            jax.ShapeDtypeStruct((3, rows, half), jnp.float32),
            jax.ShapeDtypeStruct((rows, tile), jnp.float32),
        ),
        in_specs=[vmem] * 4,
        out_specs=(vmem, vmem),
        scratch_shapes=[
            pltpu.VMEM(a_tiles.shape, jnp.bfloat16),
            pltpu.VMEM((tile, slots * tile), jnp.bfloat16),
            *[pltpu.VMEM((tile, slots * tile), jnp.bfloat16)] * 4,
            *[pltpu.VMEM((blocks_here * slots, half), jnp.int32)] * 2,
            pltpu.VMEM((3, 4, rows, half), jnp.float32),
            pltpu.VMEM((3, 3, rows, half), jnp.float32),
            pltpu.VMEM((4, rows, half), jnp.float32),
            dma((PIECES,)), dma((PIECES,)), dma((PIECES,)), dma((PIECES,)),
            dma((2,)), dma((2,)),
            dma((3, 3)), dma((3, 3)), dma((3,)), dma((3,)),
        ],
        compiler_params=pltpu.CompilerParams(
            collective_id=0, has_side_effects=True, vmem_limit_bytes=40 * 2**20),
        name="band",
    )(a_tiles, picked, meta, positions)

    row_ids = jnp.arange(rows, dtype=jnp.int32)
    pivot_block = panel[0]
    pos = pivot_block % blocks_here
    holds = group_pos == pivot_block // blocks_here
    pivot_tile = jnp.where(pos == 0, column[:tile], column[tile:])
    other_tile = jnp.where(pos == 0, column[tile:], column[:tile])
    pivot_tile = jnp.where(holds, pivot_tile, jnp.eye(tile, dtype=jnp.float32))
    factor = jnp.linalg.cholesky(pivot_tile)
    solved = lax.linalg.triangular_solve(
        factor, other_tile, left_side=False, lower=True, transpose_a=True)
    here = slab_pos % 2
    pick = lambda m, axis: lax.dynamic_slice_in_dim(m, here * half, half, axis)
    reduced = jnp.dot(
        solved, pick(solved, 0).T, precision=lax.Precision.HIGHEST,
        preferred_element_type=jnp.float32)
    in_panel = slab_pos // 2 == pos
    top = jnp.where(pos == 0, pick(factor, 1), pick(solved, 1))
    low = jnp.where(pos == 0, pick(solved, 1), pick(factor, 1))
    plane_zero = band[0]
    replaced = jnp.concatenate([top, low], axis=0)
    zero = jnp.zeros_like(reduced)
    lessened = plane_zero - jnp.concatenate(
        [jnp.where(pos == 0, zero, reduced), jnp.where(pos == 0, reduced, zero)], axis=0)
    updated = jnp.where(in_panel, replaced, lessened)
    plane_zero = jnp.where(holds, updated, plane_zero)
    return jnp.stack([plane_zero, band[1], band[2]], axis=1)


def solution(mesh):
    return jax.shard_map(
        body,
        mesh=mesh,
        in_specs=(P("blk", "slab"), P("blk", "slab", None), P("blk", "slab"), P("slab"), P()),
        out_specs=P("blk", None, "slab"),
        check_vma=False,
    )
```

```python
import functools

import jax
import jax.numpy as jnp
from jax import lax
from jax.experimental import pallas as pl
from jax.experimental.pallas import tpu as pltpu
from jax.sharding import PartitionSpec as P

ridge_shift = 0.05
MESH = pl.DeviceIdType.MESH
PIECES = 8
STRIP = 32


def split_three(value):
    high = value.astype(jnp.bfloat16)
    rest = value - high.astype(jnp.float32)
    middle = rest.astype(jnp.bfloat16)
    low = (rest - middle.astype(jnp.float32)).astype(jnp.bfloat16)
    return high, middle, low


def transposed_product(left, right):
    lh, lm, ll = split_three(left)
    rh, rm, rl = split_three(right)
    return lax.dot_general(
        jnp.concatenate([ll, lm, lh, lm, lh, lh], axis=0),
        jnp.concatenate([rh, rm, rl, rh, rm, rh], axis=0),
        (((0,), (0,)), ((), ())), preferred_element_type=jnp.float32)


def wide(value, times):
    return jnp.concatenate([value] * times, axis=1)


def factor_strip(work, upper, s):
    size = work.shape[0]
    width = work.shape[1]
    times = width // 128
    start = pl.multiple_of(s * STRIP, STRIP)
    strip = work[pl.ds(start, STRIP), :]
    row_ids = lax.broadcasted_iota(jnp.int32, (8, 128), 0)
    done = []
    rest = strip
    for g in range(STRIP // 8):
        lanes = lax.broadcasted_iota(jnp.int32, (rest.shape[0], size), 1)
        square = rest[:, :size]
        columns = []
        for j in range(8):
            hit = lanes == start + (8 * g + j)
            column = jnp.sum(jnp.where(hit, square, jnp.float32(0.0)), axis=1, keepdims=True)
            columns.append(jnp.broadcast_to(column, (rest.shape[0], 128)))
        more = rest.shape[0] > 8
        top, rest = rest[:8], rest[8:] if more else None
        tops = [c[:8] for c in columns]
        rests = [c[8:] for c in columns] if more else None
        for j in range(8):
            inverse = lax.rsqrt(tops[j][j:j + 1])
            pivot_row = top[j:j + 1] * wide(inverse, times)
            below = jnp.where(row_ids > j, tops[j] * inverse, jnp.float32(0.0))
            top = jnp.where(wide(row_ids, times) == j, pivot_row, top - wide(below, times) * pivot_row)
            if more:
                lower = rests[j] * inverse
                rest = rest - wide(lower, times) * pivot_row
            for k in range(j + 1, 8):
                entry = tops[k][j:j + 1] * inverse
                tops[k] = tops[k] - below * entry
                if more:
                    rests[k] = rests[k] - lower * entry
        done.append(top)
    rows = jnp.concatenate(done, axis=0)
    lanes = lax.broadcasted_iota(jnp.int32, rows.shape, 1)
    own = lax.broadcasted_iota(jnp.int32, rows.shape, 0) + start
    rows = jnp.where(lanes >= own, rows, jnp.float32(0.0))
    upper[pl.ds(start, STRIP), :] = rows
    work[...] -= transposed_product(rows[:, :size], rows)


def band_kernel(
    groups, slots, a_ref, picked_ref, meta_ref, pos_ref, band_ref,
    scaled, aligned, one_far, one_near, two_far, two_near, meta_one, meta_two, part, landed, gathered, work, upper,
    z_send, z_recv, x_send, x_recv, meta_send, meta_recv,
    sum_send, sum_recv, all_send, all_recv,
):
    rows = a_ref.shape[0]
    tile = rows // 2
    half = tile // 2
    piece = rows // PIECES
    per_block = PIECES // 2
    group = lax.axis_index("blk")
    slab = lax.axis_index("slab")
    chip = slab // 2
    core = slab % 2
    odd = group % 2
    ahead = (group + 2) % groups
    behind = (group + groups - 2) % groups
    across = group + 1 - 2 * odd
    mate = chip * 2 + 1 - core
    facing = (1 - chip) * 2 + core
    diagonal = (1 - chip) * 2 + 1 - core
    peers = (mate, facing, diagonal)
    far = 1 - chip
    near = chip

    barrier = pltpu.get_barrier_semaphore()
    for other in (ahead, behind, across):
        pl.semaphore_signal(barrier, inc=1, device_id=(other, slab), device_id_type=MESH)
    for other in peers:
        pl.semaphore_signal(barrier, inc=1, device_id=(group, other), device_id_type=MESH)
    pl.semaphore_wait(barrier, 6)

    def piece_rows(n):
        block = far if n < per_block else near
        return pl.ds(pl.multiple_of(block * tile + (n % per_block) * piece, piece), piece)

    def piece_of(far_ref, near_ref, n):
        start = n % per_block * piece
        return (far_ref if n < per_block else near_ref).at[start:start + piece]

    def to_ahead(n):
        return pltpu.make_async_remote_copy(
            src_ref=a_ref.at[piece_rows(n)], dst_ref=piece_of(two_far, two_near, n),
            send_sem=z_send.at[n], recv_sem=z_recv.at[n],
            device_id=(ahead, slab), device_id_type=MESH)

    def to_across(n, source):
        return pltpu.make_async_remote_copy(
            src_ref=source, dst_ref=piece_of(one_far, one_near, n),
            send_sem=x_send.at[n], recv_sem=x_recv.at[n],
            device_id=(across, slab), device_id_type=MESH)

    def meta_ahead():
        return pltpu.make_async_remote_copy(
            src_ref=meta_ref, dst_ref=meta_two, send_sem=meta_send.at[0], recv_sem=meta_recv.at[0],
            device_id=(ahead, slab), device_id_type=MESH)

    def meta_across(source):
        return pltpu.make_async_remote_copy(
            src_ref=source, dst_ref=meta_one, send_sem=meta_send.at[1], recv_sem=meta_recv.at[1],
            device_id=(across, slab), device_id_type=MESH)

    meta_ahead().start()
    for n in range(PIECES):
        to_ahead(n).start()

    @pl.when(odd == 0)
    def _():
        meta_across(meta_ref).start()
        for n in range(PIECES):
            to_across(n, a_ref.at[piece_rows(n)]).start()

    def scale_slot(i, m):
        where = (pl.ds(i * tile, tile), pl.ds(m * tile, tile))
        factors = picked_ref[i * slots + m:i * slots + m + 1, :]
        scaled[where] = (a_ref[where].astype(jnp.float32) * factors).astype(jnp.bfloat16)

    for i in range(2):
        for m in range(slots):
            scale_slot(i, m)

    def sum_copy(plane, d):
        return pltpu.make_async_remote_copy(
            src_ref=part.at[plane, peers[d]], dst_ref=landed.at[plane, d],
            send_sem=sum_send.at[plane, d], recv_sem=sum_recv.at[plane, d],
            device_id=(group, peers[d]), device_id_type=MESH)

    def multiply(plane, block, source, other_meta):
        first = pl.ds(0, tile)
        if plane == 0:
            first = pl.ds(pl.multiple_of(block * tile, tile), tile)

        def align(i):
            def one_slot(m, carry):
                mine = meta_ref[pl.ds(i * slots + m, 1), :]
                total = jnp.zeros((tile, tile), jnp.bfloat16)
                for n in range(slots):
                    theirs = other_meta[pl.ds(block * slots + n, 1), :]
                    same = jnp.where(mine == theirs, jnp.float32(1.0), jnp.float32(0.0))
                    same = jnp.concatenate([same, same], axis=1).astype(jnp.bfloat16)
                    total += source[first, n * tile:(n + 1) * tile] * same
                aligned[:, pl.ds(pl.multiple_of(m * tile, tile), tile)] = total
                return carry

            lax.fori_loop(0, slots, one_slot, 0)
            return aligned[...]

        def one(i, direct):
            here = pl.ds(pl.multiple_of(i * tile, tile), tile)
            other = source[first, :] if direct else align(i)
            total = lax.dot_general(
                scaled[here, :], other, (((1,), (1,)), ((), ())),
                preferred_element_type=jnp.float32)
            part[plane, 2 * block, here] = total[:, :half]
            part[plane, 2 * block + 1, here] = total[:, half:]

        one(block, plane == 0)
        one(1 - block, False)
        if block is far:
            sum_copy(plane, 1).start()
            sum_copy(plane, 2).start()
        else:
            sum_copy(plane, 0).start()

    def near_copies(n):
        here = pl.ds(pl.multiple_of((n - per_block) * piece, piece), piece)
        there = pl.ds(pl.multiple_of(near * tile + (n - per_block) * piece, piece), piece)
        incoming = pltpu.make_async_remote_copy(
            src_ref=a_ref.at[there], dst_ref=two_near.at[here],
            send_sem=z_send.at[n], recv_sem=z_recv.at[n],
            device_id=(ahead, slab), device_id_type=MESH)
        outgoing = pltpu.make_async_remote_copy(
            src_ref=two_near.at[here], dst_ref=one_near.at[here],
            send_sem=x_send.at[n], recv_sem=x_recv.at[n],
            device_id=(across, slab), device_id_type=MESH)
        return incoming, outgoing

    def forward_near(n):
        incoming, outgoing = near_copies(n)
        incoming.wait_recv()

        @pl.when(odd == 1)
        def _():
            outgoing.start()

    def forward(n):
        to_ahead(n).wait_recv()

        @pl.when(odd == 1)
        def _():
            to_across(n, piece_of(two_far, two_near, n)).start()

    multiply(0, far, a_ref, meta_ref)
    multiply(0, near, a_ref, meta_ref)

    meta_ahead().wait_recv()

    @pl.when(odd == 1)
    def _():
        meta_across(meta_two).start()

    forward(0)
    meta_across(meta_ref).wait_recv()

    for d in range(3):
        sum_copy(0, d).wait_recv()
    row_ids = lax.broadcasted_iota(jnp.int32, (rows, half), 0)
    col_ids = lax.broadcasted_iota(jnp.int32, (rows, half), 1) + slab * half
    ridge = jnp.where(row_ids == col_ids, jnp.float32(ridge_shift), jnp.float32(0.0))
    gathered[slab] = (part[0, slab] + landed[0, 0]) + (landed[0, 1] + landed[0, 2]) + ridge

    def all_copy(d):
        return pltpu.make_async_remote_copy(
            src_ref=gathered.at[slab], dst_ref=gathered.at[slab],
            send_sem=all_send.at[d], recv_sem=all_recv.at[d],
            device_id=(group, peers[d]), device_id_type=MESH)

    def all_arrival(d):
        return pltpu.make_async_remote_copy(
            src_ref=gathered.at[slab], dst_ref=gathered.at[peers[d]],
            send_sem=all_send.at[d], recv_sem=all_recv.at[d],
            device_id=(group, peers[d]), device_id_type=MESH)

    for d in (1, 2, 0):
        all_copy(d).start()

    for n in range(1, per_block):
        forward(n)
    multiply(2, far, two_far, meta_two)
    for d in range(3):
        all_arrival(d).wait_recv()
    pivot = pos_ref[0:1, :]
    first = (pivot & 1) == 0
    pivot_tile = jnp.concatenate(
        [jnp.where(first, gathered[h, :tile], gathered[2 + h, tile:]) for h in range(2)], axis=1)
    other_tile = jnp.concatenate(
        [jnp.where(first, gathered[h, tile:], gathered[2 + h, :tile]) for h in range(2)], axis=1)
    work[:, :tile] = jnp.float32(0.5) * (pivot_tile + pivot_tile.T)
    work[:, tile:] = other_tile.T

    strips = tile // STRIP
    quarter = strips // per_block

    def some_strips(n, carry):
        def one_strip(s, carry):
            factor_strip(work, upper, s)
            return carry

        lax.fori_loop(n * quarter, (n + 1) * quarter, one_strip, 0)

        @pl.when(n < per_block - 1)
        def _():
            forward_near(n + per_block)

        @pl.when(n == 1)
        def _():
            for p in range(per_block):
                to_across(p, piece_of(two_far, two_near, p)).wait_recv()
            multiply(1, far, one_far, meta_one)

        return carry

    lax.fori_loop(0, per_block, some_strips, 0)

    lower_half = upper[pl.ds(pl.multiple_of(core * half, half), half), :].T
    other_half = upper[:, pl.ds(pl.multiple_of(tile + core * half, half), half)]
    reduced = transposed_product(upper[:, tile:], other_half)
    top, low = gathered[slab, :tile], gathered[slab, tile:]
    in_panel = (pivot & 1) == chip
    holds = (pivot >> 1) == group
    new_top = jnp.where(
        in_panel, jnp.where(first, lower_half[:tile], lower_half[tile:]),
        jnp.where(first, top, top - reduced))
    new_low = jnp.where(
        in_panel, jnp.where(first, lower_half[tile:], lower_half[:tile]),
        jnp.where(first, low - reduced, low))
    band_ref[0, :tile] = jnp.where(holds, new_top, top)
    band_ref[0, tile:] = jnp.where(holds, new_low, low)

    forward(PIECES - 1)
    multiply(2, near, two_near, meta_two)
    for n in range(per_block, PIECES):
        to_across(n, piece_of(two_far, two_near, n)).wait_recv()
    multiply(1, near, one_near, meta_one)
    for plane in (2, 1):
        for d in range(3):
            sum_copy(plane, d).wait_recv()
        band_ref[plane] = (part[plane, slab] + landed[plane, 0]) + (
            landed[plane, 1] + landed[plane, 2])

    meta_ahead().wait_send()
    meta_across(meta_ref).wait_send()
    for n in range(PIECES):
        to_ahead(n).wait_send()
        to_across(n, piece_of(two_far, two_near, n)).wait_send()
    for d in range(3):
        all_copy(d).wait_send()
        for plane in range(3):
            sum_copy(plane, d).wait_send()


def body(a_tiles, tile_cols, tile_counts, scaling, panel):
    rows = a_tiles.shape[0]
    blocks_here = tile_cols.shape[0]
    slots = tile_cols.shape[2]
    tile = rows // blocks_here
    half = rows // 4
    col_tiles = scaling.shape[0] // tile
    groups = lax.axis_size("blk")
    cols = tile_cols[:, 0, :]
    slot_ids = jnp.arange(slots, dtype=jnp.int32)
    live = slot_ids[None, :] < tile_counts
    picked = jnp.where(live[..., None], scaling.reshape(col_tiles, tile)[cols], jnp.float32(0.0))
    picked = picked.reshape(blocks_here * slots, tile)
    meta = jnp.where(live, cols, -1).reshape(blocks_here * slots, 1)
    meta = jnp.broadcast_to(meta, (blocks_here * slots, half))
    positions = jnp.full((8, half), panel[0], jnp.int32)
    vmem = pl.BlockSpec(memory_space=pltpu.VMEM)
    dma = pltpu.SemaphoreType.DMA
    band = pl.pallas_call(
        functools.partial(band_kernel, groups, slots),
        out_shape=jax.ShapeDtypeStruct((3, rows, half), jnp.float32),
        in_specs=[vmem] * 4,
        out_specs=vmem,
        scratch_shapes=[
            pltpu.VMEM(a_tiles.shape, jnp.bfloat16),
            pltpu.VMEM((tile, slots * tile), jnp.bfloat16),
            *[pltpu.VMEM((tile, slots * tile), jnp.bfloat16)] * 4,
            *[pltpu.VMEM((blocks_here * slots, half), jnp.int32)] * 2,
            pltpu.VMEM((3, 4, rows, half), jnp.float32),
            pltpu.VMEM((3, 3, rows, half), jnp.float32),
            pltpu.VMEM((4, rows, half), jnp.float32),
            pltpu.VMEM((tile, 2 * tile), jnp.float32),
            pltpu.VMEM((tile, 2 * tile), jnp.float32),
            dma((PIECES,)), dma((PIECES,)), dma((PIECES,)), dma((PIECES,)),
            dma((2,)), dma((2,)),
            dma((3, 3)), dma((3, 3)), dma((3,)), dma((3,)),
        ],
        compiler_params=pltpu.CompilerParams(
            collective_id=0, has_side_effects=True, vmem_limit_bytes=40 * 2**20),
        name="band",
    )(a_tiles, picked, meta, positions)

    return jnp.transpose(band, (1, 0, 2))


def solution(mesh):
    return jax.shard_map(
        body,
        mesh=mesh,
        in_specs=(P("blk", "slab"), P("blk", "slab", None), P("blk", "slab"), P("slab"), P()),
        out_specs=P("blk", None, "slab"),
        check_vma=False,
    )
```

```python
import functools

import jax
import jax.numpy as jnp
from jax import lax
from jax.experimental import pallas as pl
from jax.experimental.pallas import tpu as pltpu
from jax.sharding import PartitionSpec as P

ridge_shift = 0.05
MESH = pl.DeviceIdType.MESH
PIECES = 9
STRIP = 32


def split_three(value):
    high = value.astype(jnp.bfloat16)
    rest = value - high.astype(jnp.float32)
    middle = rest.astype(jnp.bfloat16)
    low = (rest - middle.astype(jnp.float32)).astype(jnp.bfloat16)
    return high, middle, low


def transposed_product(left, right):
    lh, lm, ll = split_three(left)
    rh, rm, rl = split_three(right)
    return lax.dot_general(
        jnp.concatenate([ll, lm, lh, lm, lh, lh], axis=0),
        jnp.concatenate([rh, rm, rl, rh, rm, rh], axis=0),
        (((0,), (0,)), ((), ())), preferred_element_type=jnp.float32)


def wide(value, times):
    return jnp.concatenate([value] * times, axis=1)


def factor_strip(work, upper, s):
    size = work.shape[0]
    width = work.shape[1]
    times = width // 128
    start = pl.multiple_of(s * STRIP, STRIP)
    strip = work[pl.ds(start, STRIP), :]
    row_ids = lax.broadcasted_iota(jnp.int32, (8, 128), 0)
    done = []
    rest = strip
    for g in range(STRIP // 8):
        lanes = lax.broadcasted_iota(jnp.int32, (rest.shape[0], size), 1)
        square = rest[:, :size]
        columns = []
        for j in range(8):
            hit = lanes == start + (8 * g + j)
            column = jnp.sum(jnp.where(hit, square, jnp.float32(0.0)), axis=1, keepdims=True)
            columns.append(jnp.broadcast_to(column, (rest.shape[0], 128)))
        more = rest.shape[0] > 8
        top, rest = rest[:8], rest[8:] if more else None
        tops = [c[:8] for c in columns]
        rests = [c[8:] for c in columns] if more else None
        for j in range(8):
            inverse = lax.rsqrt(tops[j][j:j + 1])
            pivot_row = top[j:j + 1] * wide(inverse, times)
            below = jnp.where(row_ids > j, tops[j] * inverse, jnp.float32(0.0))
            top = jnp.where(wide(row_ids, times) == j, pivot_row, top - wide(below, times) * pivot_row)
            if more:
                lower = rests[j] * inverse
                rest = rest - wide(lower, times) * pivot_row
            for k in range(j + 1, 8):
                entry = tops[k][j:j + 1] * inverse
                tops[k] = tops[k] - below * entry
                if more:
                    rests[k] = rests[k] - lower * entry
        done.append(top)
    rows = jnp.concatenate(done, axis=0)
    lanes = lax.broadcasted_iota(jnp.int32, rows.shape, 1)
    own = lax.broadcasted_iota(jnp.int32, rows.shape, 0) + start
    rows = jnp.where(lanes >= own, rows, jnp.float32(0.0))
    upper[pl.ds(start, STRIP), :] = rows
    work[...] -= transposed_product(rows[:, :size], rows)


def band_kernel(
    groups, slots, a_ref, cols_ref, counts_ref, scal_ref, panel_ref, band_ref,
    own, meta_ref, picked_ref, scaled, aligned, one_far, one_near, two_far, two_near, meta_one, meta_two, part, landed, gathered, work, upper,
    z_send, z_recv, x_send, x_recv, meta_send, meta_recv, own_sem,
    sum_send, sum_recv, all_send, all_recv,
):
    rows = a_ref.shape[0]
    tile = rows // 2
    half = tile // 2
    piece = tile // 4
    far_pieces = [(n * piece, piece) for n in range(4)]
    near_pieces = far_pieces[:3] + [
        (3 * piece, piece // 2), (3 * piece + piece // 2, piece // 2)]
    per_block = len(far_pieces)
    pieces = far_pieces + near_pieces
    count = len(pieces)
    group = lax.axis_index("blk")
    slab = lax.axis_index("slab")
    chip = slab // 2
    core = slab % 2
    odd = group % 2
    ahead = (group + 2) % groups
    behind = (group + groups - 2) % groups
    across = group + 1 - 2 * odd
    mate = chip * 2 + 1 - core
    facing = (1 - chip) * 2 + core
    diagonal = (1 - chip) * 2 + 1 - core
    peers = (mate, facing, diagonal)
    far = 1 - chip
    near = chip

    own_copy = pltpu.make_async_copy(a_ref, own, own_sem.at[0])
    own_copy.start()
    barrier = pltpu.get_barrier_semaphore()
    for other in (ahead, behind, across):
        pl.semaphore_signal(barrier, inc=1, device_id=(other, slab), device_id_type=MESH)
    for other in peers:
        pl.semaphore_signal(barrier, inc=1, device_id=(group, other), device_id_type=MESH)
    for i in range(2):
        live = jnp.full((1, half), counts_ref[i, 0], jnp.int32)
        for m in range(slots):
            column = jnp.full((1, half), cols_ref[i, 0, m], jnp.int32)
            meta_ref[i * slots + m:i * slots + m + 1, :] = jnp.where(live > m, column, -1)
    entries = meta_ref[...]
    for h in range(2):
        factors = jnp.zeros((2 * slots, half), jnp.float32)
        for c in range(scal_ref.shape[0] // 2):
            factors = jnp.where(entries == c, scal_ref[2 * c + h:2 * c + h + 1, :], factors)
        picked_ref[:, h * half:(h + 1) * half] = factors
    pl.semaphore_wait(barrier, 6)

    def piece_rows(n):
        offset, size = pieces[n]
        if n < per_block:
            start = far * tile + offset
        elif offset < half:
            start = near * tile + (1 - core) * half + offset
        else:
            start = near * tile + core * half + offset - half
        return pl.ds(pl.multiple_of(start, size), size)

    def piece_of(far_ref, near_ref, n):
        offset, size = pieces[n]
        return (far_ref if n < per_block else near_ref).at[offset:offset + size]

    def to_ahead(n):
        return pltpu.make_async_remote_copy(
            src_ref=a_ref.at[piece_rows(n)], dst_ref=piece_of(two_far, two_near, n),
            send_sem=z_send.at[n], recv_sem=z_recv.at[n],
            device_id=(ahead, slab), device_id_type=MESH)

    def to_across(n, source):
        return pltpu.make_async_remote_copy(
            src_ref=source, dst_ref=piece_of(one_far, one_near, n),
            send_sem=x_send.at[n], recv_sem=x_recv.at[n],
            device_id=(across, slab), device_id_type=MESH)

    def meta_ahead():
        return pltpu.make_async_remote_copy(
            src_ref=meta_ref, dst_ref=meta_two, send_sem=meta_send.at[0], recv_sem=meta_recv.at[0],
            device_id=(ahead, slab), device_id_type=MESH)

    def meta_across(source):
        return pltpu.make_async_remote_copy(
            src_ref=source, dst_ref=meta_one, send_sem=meta_send.at[1], recv_sem=meta_recv.at[1],
            device_id=(across, slab), device_id_type=MESH)

    meta_ahead().start()
    for n in range(count):
        to_ahead(n).start()

    @pl.when(odd == 0)
    def _():
        meta_across(meta_ref).start()
        for n in range(count):
            to_across(n, a_ref.at[piece_rows(n)]).start()

    def scale_slot(i, m):
        where = (pl.ds(i * tile, tile), pl.ds(m * tile, tile))
        factors = picked_ref[i * slots + m:i * slots + m + 1, :]
        scaled[where] = (own[where].astype(jnp.float32) * factors).astype(jnp.bfloat16)

    own_copy.wait()
    for i in range(2):
        for m in range(slots):
            scale_slot(i, m)

    def sum_copy(plane, d):
        return pltpu.make_async_remote_copy(
            src_ref=part.at[plane, peers[d]], dst_ref=landed.at[plane, d],
            send_sem=sum_send.at[plane, d], recv_sem=sum_recv.at[plane, d],
            device_id=(group, peers[d]), device_id_type=MESH)

    def multiply(plane, block, source, start, size, other_meta, targets):
        first = pl.ds(start, size)

        def align(i):
            def one_slot(m, carry):
                mine = meta_ref[pl.ds(i * slots + m, 1), :]
                total = jnp.zeros((size, tile), jnp.bfloat16)
                for n in range(slots):
                    theirs = other_meta[pl.ds(block * slots + n, 1), :]
                    same = jnp.where(mine == theirs, jnp.float32(1.0), jnp.float32(0.0))
                    same = jnp.concatenate([same, same], axis=1).astype(jnp.bfloat16)
                    total += source[first, n * tile:(n + 1) * tile] * same
                aligned[:size, pl.ds(pl.multiple_of(m * tile, tile), tile)] = total
                return carry

            lax.fori_loop(0, slots, one_slot, 0)
            return aligned[:size]

        def one(i, direct):
            here = pl.ds(pl.multiple_of(i * tile, tile), tile)
            other = source[first, :] if direct else align(i)
            total = lax.dot_general(
                scaled[here, :], other, (((1,), (1,)), ((), ())),
                preferred_element_type=jnp.float32)
            if size == half:
                part[plane, 2 * block + (start_owner(targets)), here] = total
            else:
                part[plane, 2 * block, here] = total[:, :half]
                part[plane, 2 * block + 1, here] = total[:, half:]

        one(block, plane == 0)
        one(1 - block, False)
        for d in targets:
            sum_copy(plane, d).start()

    def start_owner(targets):
        return 1 - core if targets else core

    def multiply_far(plane, source, other_meta):
        multiply(plane, far, source, 0, tile, other_meta, (1, 2))

    def multiply_mate(plane, source, other_meta):
        multiply(plane, near, source, 0, half, other_meta, (0,))

    def multiply_own(plane, source, other_meta):
        multiply(plane, near, source, half, half, other_meta, ())

    def near_copies(n):
        here = pl.ds(pl.multiple_of((n - per_block) * piece, piece), piece)
        incoming = pltpu.make_async_remote_copy(
            src_ref=a_ref.at[pl.ds(0, piece)], dst_ref=two_near.at[here],
            send_sem=z_send.at[n], recv_sem=z_recv.at[n],
            device_id=(ahead, slab), device_id_type=MESH)
        outgoing = pltpu.make_async_remote_copy(
            src_ref=two_near.at[here], dst_ref=one_near.at[here],
            send_sem=x_send.at[n], recv_sem=x_recv.at[n],
            device_id=(across, slab), device_id_type=MESH)
        return incoming, outgoing

    def forward_near(n):
        incoming, outgoing = near_copies(n)
        incoming.wait_recv()

        @pl.when(odd == 1)
        def _():
            outgoing.start()

    def forward(n):
        to_ahead(n).wait_recv()

        @pl.when(odd == 1)
        def _():
            to_across(n, piece_of(two_far, two_near, n)).start()

    far_rows = pl.multiple_of(far * tile, tile)
    near_rows = pl.multiple_of(near * tile, tile)
    multiply(0, far, own, far_rows, tile, meta_ref, (1, 2))
    multiply(0, near, own, near_rows, tile, meta_ref, (0,))

    meta_ahead().wait_recv()

    @pl.when(odd == 1)
    def _():
        meta_across(meta_two).start()

    forward(0)
    meta_across(meta_ref).wait_recv()
    forward(1)

    for d in range(3):
        sum_copy(0, d).wait_recv()
    row_ids = lax.broadcasted_iota(jnp.int32, (rows, half), 0)
    col_ids = lax.broadcasted_iota(jnp.int32, (rows, half), 1) + slab * half
    ridge = jnp.where(row_ids == col_ids, jnp.float32(ridge_shift), jnp.float32(0.0))
    gathered[slab] = (part[0, slab] + landed[0, 0]) + (landed[0, 1] + landed[0, 2]) + ridge

    sent = (slab, slab, facing)

    def all_copy(d):
        return pltpu.make_async_remote_copy(
            src_ref=gathered.at[sent[d]], dst_ref=gathered.at[sent[d]],
            send_sem=all_send.at[d], recv_sem=all_recv.at[d],
            device_id=(group, (mate, facing, mate)[d]), device_id_type=MESH)

    def all_arrival(d):
        return pltpu.make_async_remote_copy(
            src_ref=gathered.at[sent[d]], dst_ref=gathered.at[peers[d]],
            send_sem=all_send.at[d], recv_sem=all_recv.at[d],
            device_id=(group, (mate, facing, mate)[d]), device_id_type=MESH)

    all_copy(1).start()
    all_copy(0).start()

    for n in range(2, per_block):
        forward(n)
    all_arrival(1).wait_recv()
    all_copy(2).start()
    multiply_far(2, two_far, meta_two)
    all_arrival(0).wait_recv()
    all_arrival(2).wait_recv()
    pivot = jnp.full((1, half), panel_ref[0], jnp.int32)
    first = (pivot & 1) == 0
    pivot_tile = jnp.concatenate(
        [jnp.where(first, gathered[h, :tile], gathered[2 + h, tile:]) for h in range(2)], axis=1)
    other_tile = jnp.concatenate(
        [jnp.where(first, gathered[h, tile:], gathered[2 + h, :tile]) for h in range(2)], axis=1)
    work[:, :tile] = jnp.float32(0.5) * (pivot_tile + pivot_tile.T)
    work[:, tile:] = other_tile.T

    strips = tile // STRIP
    quarter = strips // per_block

    def some_strips(n, carry):
        def one_strip(s, carry):
            factor_strip(work, upper, s)
            return carry

        lax.fori_loop(n * quarter, (n + 1) * quarter, one_strip, 0)

        @pl.when(n < per_block - 1)
        def _():
            forward_near(n + per_block)

        @pl.when(n == 1)
        def _():
            for p in range(per_block):
                to_across(p, piece_of(two_far, two_near, p)).wait_recv()
            multiply_far(1, one_far, meta_one)

        @pl.when(n == 2)
        def _():
            multiply_mate(2, two_near, meta_two)

        return carry

    lax.fori_loop(0, per_block, some_strips, 0)

    lower_half = upper[pl.ds(pl.multiple_of(core * half, half), half), :].T
    other_half = upper[:, pl.ds(pl.multiple_of(tile + core * half, half), half)]
    reduced = transposed_product(upper[:, tile:], other_half)
    top, low = gathered[slab, :tile], gathered[slab, tile:]
    in_panel = (pivot & 1) == chip
    holds = (pivot >> 1) == group
    new_top = jnp.where(
        in_panel, jnp.where(first, lower_half[:tile], lower_half[tile:]),
        jnp.where(first, top, top - reduced))
    new_low = jnp.where(
        in_panel, jnp.where(first, lower_half[tile:], lower_half[:tile]),
        jnp.where(first, low - reduced, low))
    band_ref[0, :tile] = jnp.where(holds, new_top, top)
    band_ref[0, tile:] = jnp.where(holds, new_low, low)

    forward(count - 2)
    forward(count - 1)
    for n in (per_block, per_block + 1):
        to_across(n, piece_of(two_far, two_near, n)).wait_recv()
    multiply_mate(1, one_near, meta_one)
    multiply_own(2, two_near, meta_two)
    for n in range(per_block + 2, count):
        to_across(n, piece_of(two_far, two_near, n)).wait_recv()
    multiply_own(1, one_near, meta_one)
    for plane in (2, 1):
        for d in range(3):
            sum_copy(plane, d).wait_recv()
        band_ref[plane] = (part[plane, slab] + landed[plane, 0]) + (
            landed[plane, 1] + landed[plane, 2])

    meta_ahead().wait_send()
    meta_across(meta_ref).wait_send()
    for n in range(count):
        to_ahead(n).wait_send()
        to_across(n, piece_of(two_far, two_near, n)).wait_send()
    for d in range(3):
        all_copy(d).wait_send()
        for plane in range(3):
            sum_copy(plane, d).wait_send()


def body(a_tiles, tile_cols, tile_counts, scaling, panel):
    rows = a_tiles.shape[0]
    blocks_here = tile_cols.shape[0]
    slots = tile_cols.shape[2]
    tile = rows // blocks_here
    half = rows // 4
    groups = lax.axis_size("blk")
    vmem = pl.BlockSpec(memory_space=pltpu.VMEM)
    smem = pl.BlockSpec(memory_space=pltpu.SMEM)
    dma = pltpu.SemaphoreType.DMA
    band = pl.pallas_call(
        functools.partial(band_kernel, groups, slots),
        out_shape=jax.ShapeDtypeStruct((3, rows, half), jnp.float32),
        in_specs=[pl.BlockSpec(memory_space=pl.ANY), smem, smem, vmem, smem],
        out_specs=vmem,
        scratch_shapes=[
            pltpu.VMEM(a_tiles.shape, jnp.bfloat16),
            pltpu.VMEM((2 * slots, half), jnp.int32),
            pltpu.VMEM((2 * slots, tile), jnp.float32),
            pltpu.VMEM(a_tiles.shape, jnp.bfloat16),
            pltpu.VMEM((tile, slots * tile), jnp.bfloat16),
            *[pltpu.VMEM((tile, slots * tile), jnp.bfloat16)] * 4,
            *[pltpu.VMEM((blocks_here * slots, half), jnp.int32)] * 2,
            pltpu.VMEM((3, 4, rows, half), jnp.float32),
            pltpu.VMEM((3, 3, rows, half), jnp.float32),
            pltpu.VMEM((4, rows, half), jnp.float32),
            pltpu.VMEM((tile, 2 * tile), jnp.float32),
            pltpu.VMEM((tile, 2 * tile), jnp.float32),
            dma((PIECES,)), dma((PIECES,)), dma((PIECES,)), dma((PIECES,)),
            dma((2,)), dma((2,)), dma((1,)),
            dma((3, 3)), dma((3, 3)), dma((3,)), dma((3,)),
        ],
        compiler_params=pltpu.CompilerParams(
            collective_id=0, has_side_effects=True, vmem_limit_bytes=60 * 2**20),
        name="band",
    )(a_tiles, tile_cols, tile_counts, scaling.reshape(-1, half), panel)

    return jnp.transpose(band, (1, 0, 2))


def solution(mesh):
    return jax.shard_map(
        body,
        mesh=mesh,
        in_specs=(P("blk", "slab"), P("blk", "slab", None), P("blk", "slab"), P("slab"), P()),
        out_specs=P("blk", None, "slab"),
        check_vma=False,
    )
```

```python
import functools

import jax
import jax.numpy as jnp
from jax import lax
from jax.experimental import pallas as pl
from jax.experimental.pallas import tpu as pltpu
from jax.sharding import PartitionSpec as P

ridge_shift = 0.05
MESH = pl.DeviceIdType.MESH
PIECES = 16
STRIP = 32


def split_three(value):
    high = value.astype(jnp.bfloat16)
    rest = value - high.astype(jnp.float32)
    middle = rest.astype(jnp.bfloat16)
    low = (rest - middle.astype(jnp.float32)).astype(jnp.bfloat16)
    return high, middle, low


def transposed_product(left, right):
    lh, lm, ll = split_three(left)
    rh, rm, rl = split_three(right)
    return lax.dot_general(
        jnp.concatenate([ll, lm, lh, lm, lh, lh], axis=0),
        jnp.concatenate([rh, rm, rl, rh, rm, rh], axis=0),
        (((0,), (0,)), ((), ())), preferred_element_type=jnp.float32)


def wide(value, times):
    return jnp.concatenate([value] * times, axis=1)


def factor_strip(work, upper, s):
    size = work.shape[0]
    width = work.shape[1]
    times = width // 128
    start = pl.multiple_of(s * STRIP, STRIP)
    strip = work[pl.ds(start, STRIP), :]
    row_ids = lax.broadcasted_iota(jnp.int32, (8, 128), 0)
    done = []
    rest = strip
    for g in range(STRIP // 8):
        lanes = lax.broadcasted_iota(jnp.int32, (rest.shape[0], size), 1)
        square = rest[:, :size]
        columns = []
        for j in range(8):
            hit = lanes == start + (8 * g + j)
            column = jnp.sum(jnp.where(hit, square, jnp.float32(0.0)), axis=1, keepdims=True)
            columns.append(jnp.broadcast_to(column, (rest.shape[0], 128)))
        more = rest.shape[0] > 8
        top, rest = rest[:8], rest[8:] if more else None
        tops = [c[:8] for c in columns]
        rests = [c[8:] for c in columns] if more else None
        for j in range(8):
            inverse = lax.rsqrt(tops[j][j:j + 1])
            pivot_row = top[j:j + 1] * wide(inverse, times)
            below = jnp.where(row_ids > j, tops[j] * inverse, jnp.float32(0.0))
            top = jnp.where(wide(row_ids, times) == j, pivot_row, top - wide(below, times) * pivot_row)
            if more:
                lower = rests[j] * inverse
                rest = rest - wide(lower, times) * pivot_row
            for k in range(j + 1, 8):
                entry = tops[k][j:j + 1] * inverse
                tops[k] = tops[k] - below * entry
                if more:
                    rests[k] = rests[k] - lower * entry
        done.append(top)
    rows = jnp.concatenate(done, axis=0)
    lanes = lax.broadcasted_iota(jnp.int32, rows.shape, 1)
    own = lax.broadcasted_iota(jnp.int32, rows.shape, 0) + start
    rows = jnp.where(lanes >= own, rows, jnp.float32(0.0))
    upper[pl.ds(start, STRIP), :] = rows
    work[...] -= transposed_product(rows[:, :size], rows)


def band_kernel(
    groups, slots, a_ref, cols_ref, counts_ref, scal_ref, panel_ref, band_ref,
    own, meta_ref, picked_ref, scaled, aligned, a_one, a_two, meta_one, meta_two, part, landed, gathered, work, upper,
    z_send, z_recv, x_send, x_recv, meta_send, meta_recv, own_sem,
    sum_send, sum_recv, all_send, all_recv,
):
    rows = a_ref.shape[0]
    tile = rows // 2
    half = tile // 2
    piece = rows // PIECES
    per_unit = PIECES // 4
    group = lax.axis_index("blk")
    slab = lax.axis_index("slab")
    chip = slab // 2
    core = slab % 2
    odd = group % 2
    ahead = (group + 2) % groups
    behind = (group + groups - 2) % groups
    across = group + 1 - 2 * odd
    mate = chip * 2 + 1 - core
    facing = (1 - chip) * 2 + core
    diagonal = (1 - chip) * 2 + 1 - core
    peers = (mate, facing, diagonal)
    far = 1 - chip
    near = chip

    own_copy = pltpu.make_async_copy(a_ref, own, own_sem.at[0])
    own_copy.start()
    barrier = pltpu.get_barrier_semaphore()
    for other in (ahead, behind, across):
        pl.semaphore_signal(barrier, inc=1, device_id=(other, slab), device_id_type=MESH)
    for other in peers:
        pl.semaphore_signal(barrier, inc=1, device_id=(group, other), device_id_type=MESH)
    for i in range(2):
        live = jnp.full((1, half), counts_ref[i], jnp.int32)
        for m in range(slots):
            column = jnp.full((1, half), cols_ref[i, 0, m], jnp.int32)
            meta_ref[i * slots + m:i * slots + m + 1, :] = jnp.where(live > m, column, -1)
    entries = meta_ref[...]
    for h in range(2):
        factors = jnp.zeros((2 * slots, half), jnp.float32)
        for c in range(scal_ref.shape[0] // 2):
            factors = jnp.where(entries == c, scal_ref[2 * c + h:2 * c + h + 1, :], factors)
        picked_ref[:, h * half:(h + 1) * half] = factors
    pl.semaphore_wait(barrier, 6)

    units = ((far, core, (1,)), (far, 1 - core, (2,)), (near, 1 - core, (0,)), (near, core, ()))

    def piece_rows(n):
        block, side, _ = units[n // per_unit]
        start = block * tile + side * half + n % per_unit * piece
        return pl.ds(pl.multiple_of(start, piece), piece)

    def landing(n):
        return pl.ds(pl.multiple_of(n * piece, piece), piece)

    def to_ahead(n, source):
        return pltpu.make_async_remote_copy(
            src_ref=source, dst_ref=a_two.at[landing(n)],
            send_sem=z_send.at[n], recv_sem=z_recv.at[n],
            device_id=(ahead, slab), device_id_type=MESH)

    def to_across(n, source):
        return pltpu.make_async_remote_copy(
            src_ref=source, dst_ref=a_one.at[landing(n)],
            send_sem=x_send.at[n], recv_sem=x_recv.at[n],
            device_id=(across, slab), device_id_type=MESH)

    some_piece = a_ref.at[pl.ds(0, piece)]

    def meta_ahead():
        return pltpu.make_async_remote_copy(
            src_ref=meta_ref, dst_ref=meta_two, send_sem=meta_send.at[0], recv_sem=meta_recv.at[0],
            device_id=(ahead, slab), device_id_type=MESH)

    def meta_across(source):
        return pltpu.make_async_remote_copy(
            src_ref=source, dst_ref=meta_one, send_sem=meta_send.at[1], recv_sem=meta_recv.at[1],
            device_id=(across, slab), device_id_type=MESH)

    meta_ahead().start()
    for n in range(PIECES):
        to_ahead(n, a_ref.at[piece_rows(n)]).start()

    @pl.when(odd == 0)
    def _():
        meta_across(meta_ref).start()
        for n in range(PIECES):
            to_across(n, a_ref.at[piece_rows(n)]).start()

    def scale_slot(i, m):
        where = (pl.ds(i * tile, tile), pl.ds(m * tile, tile))
        factors = picked_ref[i * slots + m:i * slots + m + 1, :]
        scaled[where] = (own[where].astype(jnp.float32) * factors).astype(jnp.bfloat16)

    own_copy.wait()
    for i in range(2):
        for m in range(slots):
            scale_slot(i, m)

    def sum_copy(plane, d):
        return pltpu.make_async_remote_copy(
            src_ref=part.at[plane, peers[d]], dst_ref=landed.at[plane, d],
            send_sem=sum_send.at[plane, d], recv_sem=sum_recv.at[plane, d],
            device_id=(group, peers[d]), device_id_type=MESH)

    def multiply(plane, block, source, start, size, other_meta, targets, side):
        first = pl.ds(start, size)

        def align(i):
            def one_slot(m, carry):
                mine = meta_ref[pl.ds(i * slots + m, 1), :]
                total = jnp.zeros((size, tile), jnp.bfloat16)
                for n in range(slots):
                    theirs = other_meta[pl.ds(block * slots + n, 1), :]
                    same = jnp.where(mine == theirs, jnp.float32(1.0), jnp.float32(0.0))
                    same = jnp.concatenate([same, same], axis=1).astype(jnp.bfloat16)
                    total += source[first, n * tile:(n + 1) * tile] * same
                aligned[:size, pl.ds(pl.multiple_of(m * tile, tile), tile)] = total
                return carry

            lax.fori_loop(0, slots, one_slot, 0)
            return aligned[:size]

        def one(i, direct):
            here = pl.ds(pl.multiple_of(i * tile, tile), tile)
            other = source[first, :] if direct else align(i)
            total = lax.dot_general(
                scaled[here, :], other, (((1,), (1,)), ((), ())),
                preferred_element_type=jnp.float32)
            if size == half:
                part[plane, 2 * block + side, here] = total
            else:
                part[plane, 2 * block, here] = total[:, :half]
                part[plane, 2 * block + 1, here] = total[:, half:]

        one(block, plane == 0)
        one(1 - block, False)
        for d in targets:
            sum_copy(plane, d).start()

    def multiply_unit(plane, u):
        source, other_meta = ((a_one, meta_one), (a_two, meta_two))[plane - 1]
        block, side, targets = units[u]
        if plane == 1:
            for n in range(u * per_unit, (u + 1) * per_unit):
                to_across(n, some_piece).wait_recv()
        multiply(plane, block, source, u * half, half, other_meta, targets, side)

    def forward(n):
        to_ahead(n, some_piece).wait_recv()

        @pl.when(odd == 1)
        def _():
            to_across(n, a_two.at[landing(n)]).start()

    far_rows = pl.multiple_of(far * tile, tile)
    near_rows = pl.multiple_of(near * tile, tile)
    multiply(0, far, own, far_rows, tile, meta_ref, (1, 2), 0)
    meta_ahead().wait_recv()

    @pl.when(odd == 1)
    def _():
        meta_across(meta_two).start()

    forward(0)
    multiply(0, near, own, near_rows, tile, meta_ref, (0,), 0)
    for n in (1, 2, 3):
        forward(n)
    multiply_unit(2, 0)
    meta_across(meta_ref).wait_recv()
    for d in range(3):
        sum_copy(0, d).wait_recv()
    row_ids = lax.broadcasted_iota(jnp.int32, (rows, half), 0)
    col_ids = lax.broadcasted_iota(jnp.int32, (rows, half), 1) + slab * half
    ridge = jnp.where(row_ids == col_ids, jnp.float32(ridge_shift), jnp.float32(0.0))
    gathered[slab] = (part[0, slab] + landed[0, 0]) + (landed[0, 1] + landed[0, 2]) + ridge

    sent = (slab, slab, facing)

    def all_copy(d):
        return pltpu.make_async_remote_copy(
            src_ref=gathered.at[sent[d]], dst_ref=gathered.at[sent[d]],
            send_sem=all_send.at[d], recv_sem=all_recv.at[d],
            device_id=(group, (mate, facing, mate)[d]), device_id_type=MESH)

    def all_arrival(d):
        return pltpu.make_async_remote_copy(
            src_ref=gathered.at[sent[d]], dst_ref=gathered.at[peers[d]],
            send_sem=all_send.at[d], recv_sem=all_recv.at[d],
            device_id=(group, (mate, facing, mate)[d]), device_id_type=MESH)

    all_copy(1).start()
    all_copy(0).start()

    forward(4)
    forward(5)
    multiply_unit(1, 0)
    forward(6)
    all_arrival(1).wait_recv()
    all_copy(2).start()
    forward(7)
    multiply_unit(2, 1)
    forward(8)
    all_arrival(0).wait_recv()
    all_arrival(2).wait_recv()
    pivot = jnp.full((1, half), panel_ref[0], jnp.int32)
    first = (pivot & 1) == 0
    pivot_tile = jnp.concatenate(
        [jnp.where(first, gathered[h, :tile], gathered[2 + h, tile:]) for h in range(2)], axis=1)
    other_tile = jnp.concatenate(
        [jnp.where(first, gathered[h, tile:], gathered[2 + h, :tile]) for h in range(2)], axis=1)
    work[:, :tile] = jnp.float32(0.5) * (pivot_tile + pivot_tile.T)
    work[:, tile:] = other_tile.T

    strips = tile // STRIP

    def one_strip(s, carry):
        factor_strip(work, upper, s)

        @pl.when(s < strips - 1)
        def _():
            forward(s + PIECES - strips + 1)

        @pl.when(s == 1)
        def _():
            multiply_unit(1, 1)

        @pl.when(s == 3)
        def _():
            multiply_unit(2, 2)

        @pl.when(s == 5)
        def _():
            multiply_unit(1, 2)

        return carry

    lax.fori_loop(0, strips, one_strip, 0)

    lower_half = upper[pl.ds(pl.multiple_of(core * half, half), half), :].T
    other_half = upper[:, pl.ds(pl.multiple_of(tile + core * half, half), half)]
    reduced = transposed_product(upper[:, tile:], other_half)
    top, low = gathered[slab, :tile], gathered[slab, tile:]
    in_panel = (pivot & 1) == chip
    holds = (pivot >> 1) == group
    new_top = jnp.where(
        in_panel, jnp.where(first, lower_half[:tile], lower_half[tile:]),
        jnp.where(first, top, top - reduced))
    new_low = jnp.where(
        in_panel, jnp.where(first, lower_half[tile:], lower_half[:tile]),
        jnp.where(first, low - reduced, low))
    band_ref[0, :tile] = jnp.where(holds, new_top, top)
    band_ref[0, tile:] = jnp.where(holds, new_low, low)

    multiply_unit(2, 3)
    multiply_unit(1, 3)
    for plane in (2, 1):
        for d in range(3):
            sum_copy(plane, d).wait_recv()
        band_ref[plane] = (part[plane, slab] + landed[plane, 0]) + (
            landed[plane, 1] + landed[plane, 2])

    meta_ahead().wait_send()
    meta_across(meta_ref).wait_send()
    for n in range(PIECES):
        to_ahead(n, some_piece).wait_send()
        to_across(n, some_piece).wait_send()
    for d in range(3):
        all_copy(d).wait_send()
        for plane in range(3):
            sum_copy(plane, d).wait_send()


def body(a_tiles, tile_cols, tile_counts, scaling, panel):
    rows = a_tiles.shape[0]
    blocks_here = tile_cols.shape[0]
    slots = tile_cols.shape[2]
    tile = rows // blocks_here
    half = rows // 4
    groups = lax.axis_size("blk")
    vmem = pl.BlockSpec(memory_space=pltpu.VMEM)
    smem = pl.BlockSpec(memory_space=pltpu.SMEM)
    dma = pltpu.SemaphoreType.DMA
    band = pl.pallas_call(
        functools.partial(band_kernel, groups, slots),
        out_shape=jax.ShapeDtypeStruct((3, rows, half), jnp.float32),
        in_specs=[pl.BlockSpec(memory_space=pl.ANY), smem, smem, vmem, smem],
        out_specs=vmem,
        scratch_shapes=[
            pltpu.VMEM(a_tiles.shape, jnp.bfloat16),
            pltpu.VMEM((2 * slots, half), jnp.int32),
            pltpu.VMEM((2 * slots, tile), jnp.float32),
            pltpu.VMEM(a_tiles.shape, jnp.bfloat16),
            pltpu.VMEM((tile, slots * tile), jnp.bfloat16),
            *[pltpu.VMEM(a_tiles.shape, jnp.bfloat16)] * 2,
            *[pltpu.VMEM((blocks_here * slots, half), jnp.int32)] * 2,
            pltpu.VMEM((3, 4, rows, half), jnp.float32),
            pltpu.VMEM((3, 3, rows, half), jnp.float32),
            pltpu.VMEM((4, rows, half), jnp.float32),
            pltpu.VMEM((tile, 2 * tile), jnp.float32),
            pltpu.VMEM((tile, 2 * tile), jnp.float32),
            dma((PIECES,)), dma((PIECES,)), dma((PIECES,)), dma((PIECES,)),
            dma((2,)), dma((2,)), dma((1,)),
            dma((3, 3)), dma((3, 3)), dma((3,)), dma((3,)),
        ],
        compiler_params=pltpu.CompilerParams(
            collective_id=0, has_side_effects=True, vmem_limit_bytes=52 * 2**20),
        name="band",
    )(a_tiles, tile_cols, tile_counts.reshape(-1), scaling.reshape(-1, half), panel)

    return jnp.transpose(band, (1, 0, 2))


def solution(mesh):
    return jax.shard_map(
        body,
        mesh=mesh,
        in_specs=(P("blk", "slab"), P("blk", "slab", None), P("blk", "slab"), P("slab"), P()),
        out_specs=P("blk", None, "slab"),
        check_vma=False,
    )
```

```python
import functools

import jax
import jax.numpy as jnp
from jax import lax
from jax.experimental import pallas as pl
from jax.experimental.pallas import tpu as pltpu
from jax.sharding import PartitionSpec as P

ridge_shift = 0.05
MESH = pl.DeviceIdType.MESH
PIECES = 16
STRIP = 32


def split_three(value):
    high = value.astype(jnp.bfloat16)
    rest = value - high.astype(jnp.float32)
    middle = rest.astype(jnp.bfloat16)
    low = (rest - middle.astype(jnp.float32)).astype(jnp.bfloat16)
    return high, middle, low


def transposed_product(left, right):
    lh, lm, ll = split_three(left)
    rh, rm, rl = split_three(right)
    return lax.dot_general(
        jnp.concatenate([ll, lm, lh, lm, lh, lh], axis=0),
        jnp.concatenate([rh, rm, rl, rh, rm, rh], axis=0),
        (((0,), (0,)), ((), ())), preferred_element_type=jnp.float32)


def wide(value, times):
    return jnp.concatenate([value] * times, axis=1)


def factor_strip(work, upper, s):
    size = work.shape[0]
    width = work.shape[1]
    times = width // 128
    start = pl.multiple_of(s * STRIP, STRIP)
    strip = work[pl.ds(start, STRIP), :]
    row_ids = lax.broadcasted_iota(jnp.int32, (8, 128), 0)
    done = []
    rest = strip
    for g in range(STRIP // 8):
        lanes = lax.broadcasted_iota(jnp.int32, (rest.shape[0], size), 1)
        square = rest[:, :size]
        columns = []
        for j in range(8):
            hit = lanes == start + (8 * g + j)
            column = jnp.sum(jnp.where(hit, square, jnp.float32(0.0)), axis=1, keepdims=True)
            columns.append(jnp.broadcast_to(column, (rest.shape[0], 128)))
        more = rest.shape[0] > 8
        top, rest = rest[:8], rest[8:] if more else None
        tops = [c[:8] for c in columns]
        rests = [c[8:] for c in columns] if more else None
        for j in range(8):
            inverse = lax.rsqrt(tops[j][j:j + 1])
            pivot_row = top[j:j + 1] * wide(inverse, times)
            below = jnp.where(row_ids > j, tops[j] * inverse, jnp.float32(0.0))
            top = jnp.where(wide(row_ids, times) == j, pivot_row, top - wide(below, times) * pivot_row)
            if more:
                lower = rests[j] * inverse
                rest = rest - wide(lower, times) * pivot_row
            for k in range(j + 1, 8):
                entry = tops[k][j:j + 1] * inverse
                tops[k] = tops[k] - below * entry
                if more:
                    rests[k] = rests[k] - lower * entry
        done.append(top)
    rows = jnp.concatenate(done, axis=0)
    lanes = lax.broadcasted_iota(jnp.int32, rows.shape, 1)
    own = lax.broadcasted_iota(jnp.int32, rows.shape, 0) + start
    rows = jnp.where(lanes >= own, rows, jnp.float32(0.0))
    upper[pl.ds(start, STRIP), :] = rows

    @pl.when(s < size // STRIP - 1)
    def _():
        work[...] -= transposed_product(rows[:, :size], rows)


def band_kernel(
    groups, slots, a_ref, cols_ref, counts_ref, scal_ref, panel_ref, band_ref,
    own, meta_ref, picked_ref, scaled, aligned, a_one, a_two, meta_one, meta_two, part, landed, gathered, work, upper,
    z_send, z_recv, x_send, x_recv, meta_send, meta_recv, own_sem,
    sum_send, sum_recv, all_send, all_recv,
):
    rows = a_ref.shape[0]
    tile = rows // 2
    half = tile // 2
    piece = rows // PIECES
    per_unit = PIECES // 4
    group = lax.axis_index("blk")
    slab = lax.axis_index("slab")
    chip = slab // 2
    core = slab % 2
    odd = group % 2
    ahead = (group + 2) % groups
    behind = (group + groups - 2) % groups
    across = group + 1 - 2 * odd
    mate = chip * 2 + 1 - core
    facing = (1 - chip) * 2 + core
    diagonal = (1 - chip) * 2 + 1 - core
    peers = (mate, facing, diagonal)
    far = 1 - chip
    near = chip

    own_copy = pltpu.make_async_copy(a_ref, own, own_sem.at[0])
    own_copy.start()
    barrier = pltpu.get_barrier_semaphore()
    for other in (ahead, behind, across):
        pl.semaphore_signal(barrier, inc=1, device_id=(other, slab), device_id_type=MESH)
    for other in peers:
        pl.semaphore_signal(barrier, inc=1, device_id=(group, other), device_id_type=MESH)
    for i in range(2):
        live = jnp.full((1, half), counts_ref[i], jnp.int32)
        for m in range(slots):
            column = jnp.full((1, half), cols_ref[i, 0, m], jnp.int32)
            meta_ref[i * slots + m:i * slots + m + 1, :] = jnp.where(live > m, column, -1)
    entries = meta_ref[...]
    for h in range(2):
        factors = jnp.zeros((2 * slots, half), jnp.float32)
        for c in range(scal_ref.shape[0] // 2):
            factors = jnp.where(entries == c, scal_ref[2 * c + h:2 * c + h + 1, :], factors)
        picked_ref[:, h * half:(h + 1) * half] = factors
    pl.semaphore_wait(barrier, 6)

    units = ((far, core, (1,)), (far, 1 - core, (2,)), (near, 1 - core, (0,)), (near, core, ()))

    def piece_rows(n):
        block, side, _ = units[n // per_unit]
        start = block * tile + side * half + n % per_unit * piece
        return pl.ds(pl.multiple_of(start, piece), piece)

    def landing(n):
        return pl.ds(pl.multiple_of(n * piece, piece), piece)

    def to_ahead(n, source):
        return pltpu.make_async_remote_copy(
            src_ref=source, dst_ref=a_two.at[landing(n)],
            send_sem=z_send.at[n], recv_sem=z_recv.at[n],
            device_id=(ahead, slab), device_id_type=MESH)

    def to_across(n, source):
        return pltpu.make_async_remote_copy(
            src_ref=source, dst_ref=a_one.at[landing(n)],
            send_sem=x_send.at[n], recv_sem=x_recv.at[n],
            device_id=(across, slab), device_id_type=MESH)

    some_piece = a_ref.at[pl.ds(0, piece)]

    def meta_ahead():
        return pltpu.make_async_remote_copy(
            src_ref=meta_ref, dst_ref=meta_two, send_sem=meta_send.at[0], recv_sem=meta_recv.at[0],
            device_id=(ahead, slab), device_id_type=MESH)

    def meta_across(source):
        return pltpu.make_async_remote_copy(
            src_ref=source, dst_ref=meta_one, send_sem=meta_send.at[1], recv_sem=meta_recv.at[1],
            device_id=(across, slab), device_id_type=MESH)

    meta_ahead().start()
    for n in range(PIECES):
        to_ahead(n, a_ref.at[piece_rows(n)]).start()

    @pl.when(odd == 0)
    def _():
        meta_across(meta_ref).start()
        for n in range(PIECES):
            to_across(n, a_ref.at[piece_rows(n)]).start()

    def scale_slot(i, m):
        where = (pl.ds(i * tile, tile), pl.ds(m * tile, tile))
        factors = picked_ref[i * slots + m:i * slots + m + 1, :]
        scaled[where] = (own[where].astype(jnp.float32) * factors).astype(jnp.bfloat16)

    own_copy.wait()
    for i in range(2):
        for m in range(slots):
            scale_slot(i, m)

    def sum_copy(plane, d):
        return pltpu.make_async_remote_copy(
            src_ref=part.at[plane, peers[d]], dst_ref=landed.at[plane, d],
            send_sem=sum_send.at[plane, d], recv_sem=sum_recv.at[plane, d],
            device_id=(group, peers[d]), device_id_type=MESH)

    def multiply(plane, block, source, start, size, other_meta, targets, side):
        first = pl.ds(start, size)

        def align(i):
            def one_slot(m, carry):
                mine = meta_ref[pl.ds(i * slots + m, 1), :]
                total = jnp.zeros((size, tile), jnp.bfloat16)
                for n in range(slots):
                    theirs = other_meta[pl.ds(block * slots + n, 1), :]
                    same = jnp.where(mine == theirs, jnp.float32(1.0), jnp.float32(0.0))
                    same = jnp.concatenate([same, same], axis=1).astype(jnp.bfloat16)
                    total += source[first, n * tile:(n + 1) * tile] * same
                aligned[:size, pl.ds(pl.multiple_of(m * tile, tile), tile)] = total
                return carry

            lax.fori_loop(0, slots, one_slot, 0)
            return aligned[:size]

        def one(i, direct):
            here = pl.ds(pl.multiple_of(i * tile, tile), tile)
            other = source[first, :] if direct else align(i)
            total = lax.dot_general(
                scaled[here, :], other, (((1,), (1,)), ((), ())),
                preferred_element_type=jnp.float32)
            if size == half:
                part[plane, 2 * block + side, here] = total
            else:
                part[plane, 2 * block, here] = total[:, :half]
                part[plane, 2 * block + 1, here] = total[:, half:]

        one(block, plane == 0)
        one(1 - block, False)
        for d in targets:
            sum_copy(plane, d).start()

    def multiply_unit(plane, u):
        source, other_meta = ((a_one, meta_one), (a_two, meta_two))[plane - 1]
        block, side, targets = units[u]
        if plane == 1:
            for n in range(u * per_unit, (u + 1) * per_unit):
                to_across(n, some_piece).wait_recv()
        multiply(plane, block, source, u * half, half, other_meta, targets, side)

    def forward(n):
        to_ahead(n, some_piece).wait_recv()

        @pl.when(odd == 1)
        def _():
            to_across(n, a_two.at[landing(n)]).start()

    far_rows = pl.multiple_of(far * tile, tile)
    near_rows = pl.multiple_of(near * tile, tile)
    multiply(0, far, own, far_rows, tile, meta_ref, (1, 2), 0)
    meta_ahead().wait_recv()

    @pl.when(odd == 1)
    def _():
        meta_across(meta_two).start()

    forward(0)
    multiply(0, near, own, near_rows, tile, meta_ref, (0,), 0)
    for n in (1, 2, 3):
        forward(n)
    multiply_unit(2, 0)
    meta_across(meta_ref).wait_recv()
    for d in range(3):
        sum_copy(0, d).wait_recv()
    row_ids = lax.broadcasted_iota(jnp.int32, (rows, half), 0)
    col_ids = lax.broadcasted_iota(jnp.int32, (rows, half), 1) + slab * half
    ridge = jnp.where(row_ids == col_ids, jnp.float32(ridge_shift), jnp.float32(0.0))
    gathered[slab] = (part[0, slab] + landed[0, 0]) + (landed[0, 1] + landed[0, 2]) + ridge

    sent = (slab, slab, facing)

    def all_copy(d):
        return pltpu.make_async_remote_copy(
            src_ref=gathered.at[sent[d]], dst_ref=gathered.at[sent[d]],
            send_sem=all_send.at[d], recv_sem=all_recv.at[d],
            device_id=(group, (mate, facing, mate)[d]), device_id_type=MESH)

    def all_arrival(d):
        return pltpu.make_async_remote_copy(
            src_ref=gathered.at[sent[d]], dst_ref=gathered.at[peers[d]],
            send_sem=all_send.at[d], recv_sem=all_recv.at[d],
            device_id=(group, (mate, facing, mate)[d]), device_id_type=MESH)

    all_copy(1).start()
    all_copy(0).start()

    forward(4)
    forward(5)
    multiply_unit(1, 0)
    forward(6)
    all_arrival(1).wait_recv()
    all_copy(2).start()
    forward(7)
    multiply_unit(2, 1)
    forward(8)
    all_arrival(0).wait_recv()
    all_arrival(2).wait_recv()
    pivot = jnp.full((1, half), panel_ref[0], jnp.int32)
    first = (pivot & 1) == 0
    pivot_tile = jnp.concatenate(
        [jnp.where(first, gathered[h, :tile], gathered[2 + h, tile:]) for h in range(2)], axis=1)
    other_tile = jnp.concatenate(
        [jnp.where(first, gathered[h, tile:], gathered[2 + h, :tile]) for h in range(2)], axis=1)
    work[:, :tile] = jnp.float32(0.5) * (pivot_tile + pivot_tile.T)
    work[:, tile:] = other_tile.T

    strips = tile // STRIP

    def one_strip(s, carry):
        @pl.when(s < strips - 1)
        def _():
            forward(s + PIECES - strips + 1)

        factor_strip(work, upper, s)

        @pl.when(s == 1)
        def _():
            multiply_unit(1, 1)

        @pl.when(s == 3)
        def _():
            multiply_unit(2, 2)

        return carry

    lax.fori_loop(0, strips, one_strip, 0)

    lower_half = upper[pl.ds(pl.multiple_of(core * half, half), half), :].T
    other_half = upper[:, pl.ds(pl.multiple_of(tile + core * half, half), half)]
    reduced = transposed_product(upper[:, tile:], other_half)
    top, low = gathered[slab, :tile], gathered[slab, tile:]
    in_panel = (pivot & 1) == chip
    holds = (pivot >> 1) == group
    new_top = jnp.where(
        in_panel, jnp.where(first, lower_half[:tile], lower_half[tile:]),
        jnp.where(first, top, top - reduced))
    new_low = jnp.where(
        in_panel, jnp.where(first, lower_half[tile:], lower_half[:tile]),
        jnp.where(first, low - reduced, low))
    band_ref[0, :tile] = jnp.where(holds, new_top, top)
    band_ref[0, tile:] = jnp.where(holds, new_low, low)

    multiply_unit(1, 2)
    multiply_unit(2, 3)
    multiply_unit(1, 3)
    for plane in (2, 1):
        for d in range(3):
            sum_copy(plane, d).wait_recv()
        band_ref[plane] = (part[plane, slab] + landed[plane, 0]) + (
            landed[plane, 1] + landed[plane, 2])

    meta_ahead().wait_send()
    meta_across(meta_ref).wait_send()
    for n in range(PIECES):
        to_ahead(n, some_piece).wait_send()
        to_across(n, some_piece).wait_send()
    for d in range(3):
        all_copy(d).wait_send()
        for plane in range(3):
            sum_copy(plane, d).wait_send()


def body(a_tiles, tile_cols, tile_counts, scaling, panel):
    rows = a_tiles.shape[0]
    blocks_here = tile_cols.shape[0]
    slots = tile_cols.shape[2]
    tile = rows // blocks_here
    half = rows // 4
    groups = lax.axis_size("blk")
    vmem = pl.BlockSpec(memory_space=pltpu.VMEM)
    smem = pl.BlockSpec(memory_space=pltpu.SMEM)
    dma = pltpu.SemaphoreType.DMA
    band = pl.pallas_call(
        functools.partial(band_kernel, groups, slots),
        out_shape=jax.ShapeDtypeStruct((3, rows, half), jnp.float32),
        in_specs=[pl.BlockSpec(memory_space=pl.ANY), smem, smem, vmem, smem],
        out_specs=vmem,
        scratch_shapes=[
            pltpu.VMEM(a_tiles.shape, jnp.bfloat16),
            pltpu.VMEM((2 * slots, half), jnp.int32),
            pltpu.VMEM((2 * slots, tile), jnp.float32),
            pltpu.VMEM(a_tiles.shape, jnp.bfloat16),
            pltpu.VMEM((tile, slots * tile), jnp.bfloat16),
            *[pltpu.VMEM(a_tiles.shape, jnp.bfloat16)] * 2,
            *[pltpu.VMEM((blocks_here * slots, half), jnp.int32)] * 2,
            pltpu.VMEM((3, 4, rows, half), jnp.float32),
            pltpu.VMEM((3, 3, rows, half), jnp.float32),
            pltpu.VMEM((4, rows, half), jnp.float32),
            pltpu.VMEM((tile, 2 * tile), jnp.float32),
            pltpu.VMEM((tile, 2 * tile), jnp.float32),
            dma((PIECES,)), dma((PIECES,)), dma((PIECES,)), dma((PIECES,)),
            dma((2,)), dma((2,)), dma((1,)),
            dma((3, 3)), dma((3, 3)), dma((3,)), dma((3,)),
        ],
        compiler_params=pltpu.CompilerParams(
            collective_id=0, has_side_effects=True, vmem_limit_bytes=60 * 2**20),
        name="band",
    )(a_tiles, tile_cols, tile_counts.reshape(-1), scaling.reshape(-1, half), panel)

    return jnp.transpose(band, (1, 0, 2))


def solution(mesh):
    return jax.shard_map(
        body,
        mesh=mesh,
        in_specs=(P("blk", "slab"), P("blk", "slab", None), P("blk", "slab"), P("slab"), P()),
        out_specs=P("blk", None, "slab"),
        check_vma=False,
    )
```

```python
import functools

import jax
import jax.numpy as jnp
from jax import lax
from jax.experimental import pallas as pl
from jax.experimental.pallas import tpu as pltpu
from jax.sharding import PartitionSpec as P

ridge_shift = 0.05
MESH = pl.DeviceIdType.MESH
PIECES = 16
STRIP = 32


def split_three(value):
    high = value.astype(jnp.bfloat16)
    rest = value - high.astype(jnp.float32)
    middle = rest.astype(jnp.bfloat16)
    low = (rest - middle.astype(jnp.float32)).astype(jnp.bfloat16)
    return high, middle, low


def transposed_product(left, right):
    lh, lm, ll = split_three(left)
    rh, rm, rl = split_three(right)
    return lax.dot_general(
        jnp.concatenate([ll, lm, lh, lm, lh, lh], axis=0),
        jnp.concatenate([rh, rm, rl, rh, rm, rh], axis=0),
        (((0,), (0,)), ((), ())), preferred_element_type=jnp.float32)


def wide(value, times):
    return jnp.concatenate([value] * times, axis=1)


def factor_strip(work, upper, s):
    size = work.shape[0]
    width = work.shape[1]
    times = width // 128
    start = pl.multiple_of(s * STRIP, STRIP)
    strip = work[pl.ds(start, STRIP), :]
    row_ids = lax.broadcasted_iota(jnp.int32, (8, 128), 0)
    done = []
    rest = strip
    for g in range(STRIP // 8):
        lanes = lax.broadcasted_iota(jnp.int32, (rest.shape[0], size), 1)
        square = rest[:, :size]
        columns = []
        for j in range(8):
            hit = lanes == start + (8 * g + j)
            column = jnp.sum(jnp.where(hit, square, jnp.float32(0.0)), axis=1, keepdims=True)
            columns.append(jnp.broadcast_to(column, (rest.shape[0], 128)))
        more = rest.shape[0] > 8
        top, rest = rest[:8], rest[8:] if more else None
        tops = [c[:8] for c in columns]
        rests = [c[8:] for c in columns] if more else None
        for j in range(8):
            inverse = lax.rsqrt(tops[j][j:j + 1])
            pivot_row = top[j:j + 1] * wide(inverse, times)
            below = jnp.where(row_ids > j, tops[j] * inverse, jnp.float32(0.0))
            top = jnp.where(wide(row_ids, times) == j, pivot_row, top - wide(below, times) * pivot_row)
            if more:
                lower = rests[j] * inverse
                rest = rest - wide(lower, times) * pivot_row
            for k in range(j + 1, 8):
                entry = tops[k][j:j + 1] * inverse
                tops[k] = tops[k] - below * entry
                if more:
                    rests[k] = rests[k] - lower * entry
        done.append(top)
    rows = jnp.concatenate(done, axis=0)
    lanes = lax.broadcasted_iota(jnp.int32, rows.shape, 1)
    own = lax.broadcasted_iota(jnp.int32, rows.shape, 0) + start
    rows = jnp.where(lanes >= own, rows, jnp.float32(0.0))
    upper[pl.ds(start, STRIP), :] = rows

    @pl.when(s < size // STRIP - 1)
    def _():
        work[...] -= transposed_product(rows[:, :size], rows)


def band_kernel(
    groups, slots, a_ref, cols_ref, counts_ref, scal_ref, panel_ref, band_ref,
    own, meta_ref, picked_ref, scaled, aligned, a_one, a_two, meta_one, meta_two, part, landed, gathered, work, upper,
    z_send, z_recv, x_send, x_recv, meta_send, meta_recv, own_sem,
    sum_send, sum_recv, all_send, all_recv,
):
    rows = a_ref.shape[0]
    tile = rows // 2
    half = tile // 2
    piece = rows // PIECES
    per_unit = PIECES // 4
    group = lax.axis_index("blk")
    slab = lax.axis_index("slab")
    chip = slab // 2
    core = slab % 2
    odd = group % 2
    ahead = (group + 2) % groups
    behind = (group + groups - 2) % groups
    across = group + 1 - 2 * odd
    mate = chip * 2 + 1 - core
    facing = (1 - chip) * 2 + core
    diagonal = (1 - chip) * 2 + 1 - core
    peers = (mate, facing, diagonal)
    far = 1 - chip
    near = chip

    own_copy = pltpu.make_async_copy(a_ref, own, own_sem.at[0])
    own_copy.start()
    barrier = pltpu.get_barrier_semaphore()
    for other in (ahead, behind, across):
        pl.semaphore_signal(barrier, inc=1, device_id=(other, slab), device_id_type=MESH)
    for other in peers:
        pl.semaphore_signal(barrier, inc=1, device_id=(group, other), device_id_type=MESH)
    for i in range(2):
        live = jnp.full((1, half), counts_ref[i], jnp.int32)
        for m in range(slots):
            column = jnp.full((1, half), cols_ref[i, 0, m], jnp.int32)
            meta_ref[i * slots + m:i * slots + m + 1, :] = jnp.where(live > m, column, -1)
    entries = meta_ref[...]
    for h in range(2):
        factors = jnp.zeros((2 * slots, half), jnp.float32)
        for c in range(scal_ref.shape[0] // 2):
            factors = jnp.where(entries == c, scal_ref[2 * c + h:2 * c + h + 1, :], factors)
        picked_ref[:, h * half:(h + 1) * half] = factors
    pl.semaphore_wait(barrier, 6)

    units = ((far, core, (1,)), (far, 1 - core, (2,)), (near, 1 - core, (0,)), (near, core, ()))

    def piece_rows(n):
        block, side, _ = units[n // per_unit]
        start = block * tile + side * half + n % per_unit * piece
        return pl.ds(pl.multiple_of(start, piece), piece)

    def landing(n):
        return pl.ds(pl.multiple_of(n * piece, piece), piece)

    def to_ahead(n, source):
        return pltpu.make_async_remote_copy(
            src_ref=source, dst_ref=a_two.at[landing(n)],
            send_sem=z_send.at[n], recv_sem=z_recv.at[n],
            device_id=(ahead, slab), device_id_type=MESH)

    def to_across(n, source):
        return pltpu.make_async_remote_copy(
            src_ref=source, dst_ref=a_one.at[landing(n)],
            send_sem=x_send.at[n], recv_sem=x_recv.at[n],
            device_id=(across, slab), device_id_type=MESH)

    some_piece = a_ref.at[pl.ds(0, piece)]

    def meta_ahead():
        return pltpu.make_async_remote_copy(
            src_ref=meta_ref, dst_ref=meta_two, send_sem=meta_send.at[0], recv_sem=meta_recv.at[0],
            device_id=(ahead, slab), device_id_type=MESH)

    def meta_across(source):
        return pltpu.make_async_remote_copy(
            src_ref=source, dst_ref=meta_one, send_sem=meta_send.at[1], recv_sem=meta_recv.at[1],
            device_id=(across, slab), device_id_type=MESH)

    meta_ahead().start()
    for n in range(PIECES):
        to_ahead(n, a_ref.at[piece_rows(n)]).start()

    @pl.when(odd == 0)
    def _():
        meta_across(meta_ref).start()
        for n in range(PIECES):
            to_across(n, a_ref.at[piece_rows(n)]).start()

    def scale_slot(i, m):
        where = (pl.ds(i * tile, tile), pl.ds(m * tile, tile))
        factors = picked_ref[i * slots + m:i * slots + m + 1, :]
        scaled[where] = (own[where].astype(jnp.float32) * factors).astype(jnp.bfloat16)

    own_copy.wait()
    for i in range(2):
        for m in range(slots):
            scale_slot(i, m)

    def sum_copy(plane, d):
        return pltpu.make_async_remote_copy(
            src_ref=part.at[plane, peers[d]], dst_ref=landed.at[plane, d],
            send_sem=sum_send.at[plane, d], recv_sem=sum_recv.at[plane, d],
            device_id=(group, peers[d]), device_id_type=MESH)

    def multiply(plane, block, source, start, size, other_meta, targets, side):
        first = pl.ds(start, size)

        def align(i):
            def one_slot(m, carry):
                mine = meta_ref[pl.ds(i * slots + m, 1), :]
                total = jnp.zeros((size, tile), jnp.bfloat16)
                for n in range(slots):
                    theirs = other_meta[pl.ds(block * slots + n, 1), :]
                    same = jnp.where(mine == theirs, jnp.float32(1.0), jnp.float32(0.0))
                    same = jnp.concatenate([same, same], axis=1).astype(jnp.bfloat16)
                    total += source[first, n * tile:(n + 1) * tile] * same
                aligned[:size, pl.ds(pl.multiple_of(m * tile, tile), tile)] = total
                return carry

            lax.fori_loop(0, slots, one_slot, 0)
            return aligned[:size]

        def one(i, direct):
            here = pl.ds(pl.multiple_of(i * tile, tile), tile)
            other = source[first, :] if direct else align(i)
            total = lax.dot_general(
                scaled[here, :], other, (((1,), (1,)), ((), ())),
                preferred_element_type=jnp.float32)
            if size == half:
                part[plane, 2 * block + side, here] = total
            else:
                part[plane, 2 * block, here] = total[:, :half]
                part[plane, 2 * block + 1, here] = total[:, half:]

        one(block, plane == 0)
        one(1 - block, False)
        for d in targets:
            sum_copy(plane, d).start()

    def multiply_unit(plane, u):
        source, other_meta = ((a_one, meta_one), (a_two, meta_two))[plane - 1]
        block, side, targets = units[u]
        if plane == 1:
            for n in range(u * per_unit, (u + 1) * per_unit):
                to_across(n, some_piece).wait_recv()
        multiply(plane, block, source, u * half, half, other_meta, targets, side)

    def forward(n):
        to_ahead(n, some_piece).wait_recv()

        @pl.when(odd == 1)
        def _():
            to_across(n, a_two.at[landing(n)]).start()

    far_rows = pl.multiple_of(far * tile, tile)
    near_rows = pl.multiple_of(near * tile, tile)
    multiply(0, far, own, far_rows, tile, meta_ref, (1, 2), 0)
    meta_ahead().wait_recv()

    @pl.when(odd == 1)
    def _():
        meta_across(meta_two).start()

    forward(0)
    multiply(0, near, own, near_rows, tile, meta_ref, (0,), 0)
    for n in (1, 2, 3):
        forward(n)
    multiply_unit(2, 0)
    meta_across(meta_ref).wait_recv()
    for d in range(3):
        sum_copy(0, d).wait_recv()
    row_ids = lax.broadcasted_iota(jnp.int32, (rows, half), 0)
    col_ids = lax.broadcasted_iota(jnp.int32, (rows, half), 1) + slab * half
    ridge = jnp.where(row_ids == col_ids, jnp.float32(ridge_shift), jnp.float32(0.0))
    gathered[slab] = (part[0, slab] + landed[0, 0]) + (landed[0, 1] + landed[0, 2]) + ridge

    sent = (slab, slab, facing)

    def all_copy(d):
        return pltpu.make_async_remote_copy(
            src_ref=gathered.at[sent[d]], dst_ref=gathered.at[sent[d]],
            send_sem=all_send.at[d], recv_sem=all_recv.at[d],
            device_id=(group, (mate, facing, mate)[d]), device_id_type=MESH)

    def all_arrival(d):
        return pltpu.make_async_remote_copy(
            src_ref=gathered.at[sent[d]], dst_ref=gathered.at[peers[d]],
            send_sem=all_send.at[d], recv_sem=all_recv.at[d],
            device_id=(group, (mate, facing, mate)[d]), device_id_type=MESH)

    all_copy(1).start()
    all_copy(0).start()

    forward(4)
    forward(5)
    multiply_unit(1, 0)
    forward(6)
    all_arrival(1).wait_recv()
    all_copy(2).start()
    forward(7)
    multiply_unit(2, 1)
    forward(8)
    all_arrival(0).wait_recv()
    all_arrival(2).wait_recv()
    pivot = jnp.full((1, half), panel_ref[0], jnp.int32)
    first = (pivot & 1) == 0
    pivot_tile = jnp.concatenate(
        [jnp.where(first, gathered[h, :tile], gathered[2 + h, tile:]) for h in range(2)], axis=1)
    other_tile = jnp.concatenate(
        [jnp.where(first, gathered[h, tile:], gathered[2 + h, :tile]) for h in range(2)], axis=1)
    work[:, :tile] = jnp.float32(0.5) * (pivot_tile + pivot_tile.T)
    work[:, tile:] = other_tile.T

    strips = tile // STRIP

    def one_strip(s, carry):
        factor_strip(work, upper, s)

        @pl.when(s < strips - 1)
        def _():
            forward(s + PIECES - strips + 1)

        @pl.when(s == 1)
        def _():
            multiply_unit(1, 1)

        @pl.when(s == 3)
        def _():
            multiply_unit(2, 2)

        @pl.when(s == 5)
        def _():
            multiply_unit(1, 2)

        return carry

    lax.fori_loop(0, strips, one_strip, 0)

    lower_half = upper[pl.ds(pl.multiple_of(core * half, half), half), :].T
    other_half = upper[:, pl.ds(pl.multiple_of(tile + core * half, half), half)]
    reduced = transposed_product(upper[:, tile:], other_half)
    top, low = gathered[slab, :tile], gathered[slab, tile:]
    in_panel = (pivot & 1) == chip
    holds = (pivot >> 1) == group
    new_top = jnp.where(
        in_panel, jnp.where(first, lower_half[:tile], lower_half[tile:]),
        jnp.where(first, top, top - reduced))
    new_low = jnp.where(
        in_panel, jnp.where(first, lower_half[tile:], lower_half[:tile]),
        jnp.where(first, low - reduced, low))
    band_ref[0, :tile] = jnp.where(holds, new_top, top)
    band_ref[0, tile:] = jnp.where(holds, new_low, low)

    multiply_unit(2, 3)
    multiply_unit(1, 3)
    for plane in (2, 1):
        for d in range(3):
            sum_copy(plane, d).wait_recv()
        band_ref[plane] = (part[plane, slab] + landed[plane, 0]) + (
            landed[plane, 1] + landed[plane, 2])

    meta_ahead().wait_send()
    meta_across(meta_ref).wait_send()
    for n in range(PIECES):
        to_ahead(n, some_piece).wait_send()
        to_across(n, some_piece).wait_send()
    for d in range(3):
        all_copy(d).wait_send()
        for plane in range(3):
            sum_copy(plane, d).wait_send()


def body(a_tiles, tile_cols, tile_counts, scaling, panel):
    rows = a_tiles.shape[0]
    blocks_here = tile_cols.shape[0]
    slots = tile_cols.shape[2]
    tile = rows // blocks_here
    half = rows // 4
    groups = lax.axis_size("blk")
    vmem = pl.BlockSpec(memory_space=pltpu.VMEM)
    smem = pl.BlockSpec(memory_space=pltpu.SMEM)
    dma = pltpu.SemaphoreType.DMA
    band = pl.pallas_call(
        functools.partial(band_kernel, groups, slots),
        out_shape=jax.ShapeDtypeStruct((3, rows, half), jnp.float32),
        in_specs=[pl.BlockSpec(memory_space=pl.ANY), smem, smem, vmem, smem],
        out_specs=vmem,
        scratch_shapes=[
            pltpu.VMEM(a_tiles.shape, jnp.bfloat16),
            pltpu.VMEM((2 * slots, half), jnp.int32),
            pltpu.VMEM((2 * slots, tile), jnp.float32),
            pltpu.VMEM(a_tiles.shape, jnp.bfloat16),
            pltpu.VMEM((tile, slots * tile), jnp.bfloat16),
            *[pltpu.VMEM(a_tiles.shape, jnp.bfloat16)] * 2,
            *[pltpu.VMEM((blocks_here * slots, half), jnp.int32)] * 2,
            pltpu.VMEM((3, 4, rows, half), jnp.float32),
            pltpu.VMEM((3, 3, rows, half), jnp.float32),
            pltpu.VMEM((4, rows, half), jnp.float32),
            pltpu.VMEM((tile, 2 * tile), jnp.float32),
            pltpu.VMEM((tile, 2 * tile), jnp.float32),
            dma((PIECES,)), dma((PIECES,)), dma((PIECES,)), dma((PIECES,)),
            dma((2,)), dma((2,)), dma((1,)),
            dma((3, 3)), dma((3, 3)), dma((3,)), dma((3,)),
        ],
        compiler_params=pltpu.CompilerParams(
            collective_id=0, has_side_effects=True, vmem_limit_bytes=60 * 2**20),
        name="band",
    )(a_tiles, tile_cols, tile_counts.reshape(-1), scaling.reshape(-1, half), panel)

    return jnp.transpose(band, (1, 0, 2))


def solution(mesh):
    return jax.shard_map(
        body,
        mesh=mesh,
        in_specs=(P("blk", "slab"), P("blk", "slab", None), P("blk", "slab"), P("slab"), P()),
        out_specs=P("blk", None, "slab"),
        check_vma=False,
    )
```
